1024 devices in a mesh: dp: 64 (over z, core), etp: 16 (over x, y).
Axes of the slice: x: 4, y: 4, z: 32, core: 2. Of those that a mesh axis runs over, the one named last changes fastest.
Arguments:
- tokens: bfloat16 [1024, 3072], P('dp', 'etp'), may hold values from -6 to 6
- upstream: bfloat16 [1024, 3072], P('dp', 'etp'), may hold values from -6 to 6
- route_ids: int32 [1024, 2], P('dp'), may hold values from 0 to 7, all different within a row; in each aligned block of 16 rows (0 to 15, 16 to 31, ...) at most 8 rows name the same one
- route_weights: float32 [1024, 2], P('dp'), may hold values from 0.1 to 1
- w_gate: bfloat16 [3072, 131072], P(None, ('dp', 'etp')), may hold values from -0.109375 to 0.109375
- w_up: bfloat16 [3072, 131072], P(None, ('dp', 'etp')), may hold values from -0.109375 to 0.109375
- w_down: bfloat16 [131072, 3072], P(('dp', 'etp')), may hold values from -0.046875 to 0.046875
Outputs:
- grad_tokens: float32 [1024, 3072], P('dp', 'etp')
The draws below stay inside these ranges and needn't reach their ends.
Inputs may be any that keep to these rules, and one draw needn't show every extreme that they name: `route_ids`: among the 16 tokens of one index of dp no expert is named by more than 8 tokens; in some of them one expert is named by exactly 8.
All inputs are finite; a program needn't handle non-finite values.
Results may differ from the reference program's by a relative error of at most 0.004.
Values may be sent and summed in bfloat16 or wider, within the bound.
A program may use at most 64 MiB of HBM per device.

```python
import math
import jax
import jax.numpy as jnp
import numpy as np
from jax import lax

D = 3072
FF = 16384
EXPERTS = 8
TOK_DEV = 16
CAP = 8
TOKENS = 1024


def level_of(key, dims, cuts, low, high):
    def one(dim, blocks):
        steps = jax.random.uniform(jax.random.fold_in(jax.random.fold_in(key, 6), dim), (blocks,), jnp.float32, low / len(cuts), high / len(cuts))
        return jnp.repeat(jnp.exp(steps), dims[dim] // blocks).reshape((-1,) + (1,) * (len(dims) - dim - 1))

    gain = one(*cuts[0])
    for cut in cuts[1:]:
        gain = gain * one(*cut)
    return gain


def shared_out(own_key, own, number, rows, amount, top, most, skew):
    sequence = jax.random.permutation(own_key, amount)
    packed, usual = load_shares(amount, rows * top, most, skew, True), load_shares(amount, rows * top, most, skew, False)
    places = jnp.arange(amount)

    def named(lengths, offset_by):
        used = int((lengths > 0).sum())
        fixed = max(1, used // 4)
        passed = fixed + (places - fixed + offset_by * (used - fixed)) % max(1, amount - fixed)
        return jnp.zeros((amount,), jnp.int32).at[sequence[jnp.where(places < fixed, places, passed)]].set(jnp.asarray(lengths, jnp.int32))

    lengths = jnp.where(number % 4 == 0, named(packed, number // 4), named(usual, number - number // 4 - 1))
    mixed = jax.random.permutation(jax.random.fold_in(own, 3), amount)
    source_of, sink = mixed[0:amount // 2 * 2:2], mixed[1:amount // 2 * 2:2]
    room = jnp.minimum(lengths[source_of] - 1, most - lengths[sink]) // 2
    room = jnp.where((source_of == sequence[0]) | (sink == sequence[0]) | (lengths[sink] == 0), 0, jnp.maximum(room, 0))
    passed = jax.random.randint(jax.random.fold_in(own, 4), (amount // 2,), 0, 1 << 20) % (room + 1)
    lengths = lengths.at[source_of].add(-passed).at[sink].add(passed)
    labels = jnp.searchsorted(jnp.cumsum(lengths), jnp.arange(rows * top), side="right").astype(jnp.int32)
    grid = labels.reshape(top, rows).T
    grid = grid[jax.random.permutation(jax.random.fold_in(own, 1), rows)]
    offset_by = jax.random.randint(jax.random.fold_in(own, 2), (rows, 1), 0, top)
    return jnp.take_along_axis(grid, (jnp.arange(top)[None, :] + offset_by) % top, axis=1)


def load_shares(number_of, total, bound, lean, full):
    portions = [(1 << 20) // math.isqrt(standing ** lean) + 1 for standing in range(1, number_of + 1)]
    largest = bound if full else min(bound, max(-(-total // number_of), total * portions[0] // sum(portions)))
    least = 1 if total - largest >= number_of - 1 else 0
    given, spare = [largest] + [least] * (number_of - 1), total - largest - least * (number_of - 1)
    while spare > 0:
        movable = [i for i in range(1, number_of) if given[i] < largest] or [i for i in range(1, number_of) if given[i] < bound]
        pool, remaining = sum([portions[i] for i in movable]), spare
        for i in movable:
            more = min(bound - given[i], max(1, remaining * portions[i] // pool), spare)
            given[i] = given[i] + more
            spare = spare - more
    return np.array(given)


def gaussian(key, extent, scale, most, pieces=(), kind=jnp.bfloat16):
    entries = scale * jax.random.normal(key, extent, jnp.float32)
    if pieces:
        entries = entries * level_of(key, extent, pieces, -0.22, 0.18)
    return jnp.clip(entries, -most, most).astype(kind)


def setup_inputs(seed: int = 0) -> dict:
    key_list = jax.random.split(jax.random.key(seed), 8)
    tokens = gaussian(key_list[0], (TOKENS, D), 1.0, 6.0, ((0, 64), (1, 16)))
    upstream = gaussian(key_list[1], (TOKENS, D), 1.0, 6.0, ((0, 64), (1, 16)))
    route_ids_keys = jax.random.split(jax.random.fold_in(key_list[2], 1), TOKENS // TOK_DEV)
    route_ids_turns = jax.random.permutation(jax.random.fold_in(key_list[2], 3), TOKENS // TOK_DEV)
    route_ids = jax.vmap(lambda own, number: shared_out(jax.random.fold_in(key_list[2], 2), own, number, TOK_DEV, EXPERTS, 2, CAP, 2))(route_ids_keys, route_ids_turns).reshape((TOKENS, 2))
    route_weights = jnp.clip(0.1 + 0.9 * jax.random.uniform(key_list[3], (TOKENS, 2), jnp.float32) ** level_of(key_list[3], (TOKENS, 2), ((0, 64),), -0.2, 0.2), 0.1, 1.0)
    w_gate = gaussian(key_list[4], (D, EXPERTS * FF), D ** -0.5, 0.109375, ((1, 1024),))
    w_up = gaussian(key_list[5], (D, EXPERTS * FF), D ** -0.5, 0.109375, ((1, 1024),))
    w_down = gaussian(key_list[6], (EXPERTS * FF, D), FF ** -0.5, 0.046875, ((0, 1024),))
    return {"tokens": tokens, "upstream": upstream, "route_ids": route_ids, "route_weights": route_weights, "w_gate": w_gate, "w_up": w_up, "w_down": w_down}


def reference(tokens, upstream, route_ids, route_weights, w_gate, w_up, w_down):
    scaled = (route_weights[:, :, None] * upstream[:, None, :].astype(jnp.float32)).astype(jnp.bfloat16)

    def one_expert(total, expert):
        chosen = route_ids == expert
        dy_rows = jnp.sum(jnp.where(chosen[:, :, None], scaled.astype(jnp.float32), 0.0), axis=1).astype(jnp.bfloat16)
        gate_cols = lax.dynamic_slice_in_dim(w_gate, expert * FF, FF, 1)
        up_cols = lax.dynamic_slice_in_dim(w_up, expert * FF, FF, 1)
        down_rows = lax.dynamic_slice_in_dim(w_down, expert * FF, FF, 0)
        gate_pre = jnp.dot(tokens, gate_cols, preferred_element_type=jnp.float32)
        up_pre = jnp.dot(tokens, up_cols, preferred_element_type=jnp.float32)
        back_grad = lax.dot_general(dy_rows, down_rows, (((1,), (1,)), ((), ())), preferred_element_type=jnp.float32)
        sigmoid_gate = jax.nn.sigmoid(gate_pre)
        d_gate = (back_grad * up_pre * sigmoid_gate * (1.0 + gate_pre * (1.0 - sigmoid_gate))).astype(jnp.bfloat16)
        d_up = (back_grad * gate_pre * sigmoid_gate).astype(jnp.bfloat16)
        term = lax.dot_general(d_gate, gate_cols, (((1,), (1,)), ((), ())), preferred_element_type=jnp.float32)
        term = term + lax.dot_general(d_up, up_cols, (((1,), (1,)), ((), ())), preferred_element_type=jnp.float32)
        return total + term, None

    start_sum = jnp.zeros(tokens.shape, jnp.float32)
    total, unused = lax.scan(one_expert, start_sum, jnp.arange(EXPERTS, dtype=jnp.int32))
    return total
```

```python
import functools

import jax
import jax.numpy as jnp
from jax import lax
from jax.experimental import pallas as pl
from jax.experimental.pallas import tpu as pltpu
from jax.sharding import PartitionSpec as P

EXPERTS = 8
CORES = 2
RING = 4
WIN = 256
F32 = jnp.float32
BF16 = jnp.bfloat16
MESH = pl.DeviceIdType.MESH


def nn(a, b, precision=None):
    return lax.dot_general(a, b, (((1,), (0,)), ((), ())), preferred_element_type=F32, precision=precision)


def nt(a, b):
    return lax.dot_general(a, b, (((1,), (1,)), ((), ())), preferred_element_type=F32)


def tn(a, b):
    return lax.dot_general(a, b, (((0,), (0,)), ((), ())), preferred_element_type=F32)


def kernel(
    zl_n,
    tok_ref, up_ref, ids_ref, rw_ref, wg_hbm, wu_hbm, wd_hbm,
    out_ref,
    wg, wu, wd, blk, zbuf, zfull, dgu, sbuf, relay, main, tsum, thalf, relay2, main2, fsum, fhalf, zrecv, vsum, rfin,
    load_sem, send_sem, recv_sem,
):
    src_n = zl_n * EXPERTS
    half_src = src_n // 2
    tok, feat = tok_ref.shape
    cap = tok // 2
    dp, etp = lax.axis_index("dp"), lax.axis_index("etp")
    core, z = dp % CORES, dp // CORES
    zl, e = z % zl_n, z // zl_n
    x, y = etp // RING, etp % RING
    odd = etp % 2
    counter = [0]
    started = []

    def at_dp(zz, cc):
        return {"dp": zz * CORES + cc}

    def at_xy(xx, yy):
        return {"etp": xx * RING + yy}

    def send(src, dst, device):
        k = counter[0]
        counter[0] += 1
        cp = pltpu.make_async_remote_copy(
            src_ref=src, dst_ref=dst, send_sem=send_sem.at[k], recv_sem=recv_sem.at[k], device_id=device,
            device_id_type=MESH,
        )
        cp.start()
        started.append(cp)
        return cp

    hid = wg_hbm.shape[1]
    loads = [
        pltpu.make_async_copy(wg_hbm, wg.at[:, 0:hid], load_sem.at[0]),
        pltpu.make_async_copy(wu_hbm, wu.at[:, 0:hid], load_sem.at[1]),
        pltpu.make_async_copy(wd_hbm, wd.at[0:hid, :], load_sem.at[2]),
    ]
    for cp in loads:
        cp.start()

    partners = [at_dp(z, 1 - core)]
    partners += [at_dp((e + d) % EXPERTS * zl_n + zl, core) for d in range(1, EXPERTS)]
    partners += [at_dp(e * zl_n + (zl + d) % zl_n, core) for d in range(1, zl_n)]
    partners += [at_xy((x + d) % RING, y) for d in (1, RING - 1)]
    partners += [at_xy(x, (y + d) % RING) for d in (1, RING - 1)]
    barrier = pltpu.get_barrier_semaphore()
    for device in partners:
        pl.semaphore_signal(barrier, inc=1, device_id=device, device_id_type=MESH)

    lane = lax.broadcasted_iota(jnp.int32, (tok, EXPERTS * cap), 1)
    lane_e, lane_s = lane >> 3, lane & 7
    ids = ids_ref[...]
    hit0, hit1 = ids[:, 0:1] == lane_e, ids[:, 1:2] == lane_e
    one0, one1 = jnp.where(hit0, 1.0, 0.0).astype(F32), jnp.where(hit1, 1.0, 0.0).astype(F32)
    lower = lax.broadcasted_iota(jnp.int32, (tok, tok), 1) < lax.broadcasted_iota(jnp.int32, (tok, tok), 0)
    before = nn(jnp.where(lower, 1.0, 0.0).astype(F32), one0 + one1)
    slot_ok = jnp.where(before == lane_s.astype(F32), 1.0, 0.0).astype(F32)
    p0, p1 = one0 * slot_ok, one1 * slot_ok
    placed = p0 + p1
    shift = lax.broadcasted_iota(jnp.int32, (feat, WIN), 1) - lax.broadcasted_iota(jnp.int32, (feat, WIN), 0)
    spread = jnp.where(shift == odd * (WIN - feat), 1.0, 0.0).astype(BF16)
    xw = nn(tok_ref[...], spread).astype(BF16)
    uw = nn(up_ref[...], spread)
    rw = rw_ref[...]
    d0, d1 = (rw[:, 0:1] * uw).astype(BF16), (rw[:, 1:2] * uw).astype(BF16)
    xs = tn(placed.astype(BF16), xw).reshape(EXPERTS, cap, WIN)
    ds = (tn(p0.astype(BF16), d0) + tn(p1.astype(BF16), d1)).reshape(EXPERTS, cap, WIN)
    blk[...] = jnp.concatenate([xs, ds], axis=1).astype(BF16)

    pl.semaphore_wait(barrier, len(partners))

    half = zl // (zl_n // 2)
    pa, pb = x + half * (y - x), y + half * (x - y)
    zrow = pl.multiple_of(zl % (zl_n // 2) * (EXPERTS * tok), EXPERTS * tok)
    mine = zbuf.at[half, pa, pb, pl.ds(pl.multiple_of(zrow + e * tok, tok), tok)]
    own = pltpu.make_async_copy(blk.at[e], mine, load_sem.at[3])
    own.start()
    moves = []
    for d in range(1, EXPERTS):
        to = (e + d) % EXPERTS
        moves.append(send(blk.at[to], mine, at_dp(to * zl_n + zl, core)))
    sibling = at_dp(z, 1 - core)
    weights = [
        send(wd_hbm, wd.at[hid:, :], sibling),
        send(wg_hbm, wg.at[:, hid:], sibling),
        send(wu_hbm, wu.at[:, hid:], sibling),
    ]
    own.wait()
    for cp in moves:
        cp.wait_recv()
    region = zbuf.at[half, pa, pb, pl.ds(zrow, EXPERTS * tok)]
    moves = [send(region, region, at_dp(e * zl_n + (zl + d) % zl_n, core)) for d in range(1, zl_n)]
    for cp in moves:
        cp.wait_recv()

    def ahead(h, stage, step):
        if (h == 0) == (stage == 0):
            return at_xy((x + step) % RING, y)
        return at_xy(x, (y + step) % RING)

    def place(h):
        return (x, y) if h == 0 else (y, x)

    rows = half_src * tok
    lo, hi = slice(0, rows // 2), slice(rows // 2, rows)

    def block(h, stage, step, part):
        a, b = place(h)
        if stage == 0:
            return zbuf.at[h, (a + step + RING) % RING, b, part]
        return zbuf.at[h, :, (b + step + RING) % RING, part]

    for stage in range(2):
        first = []
        for h in range(2):
            first.append([
                send(block(h, stage, 0, lo), block(h, stage, 0, lo), ahead(h, stage, 1)),
                send(block(h, stage, 0, hi), block(h, stage, 0, hi), ahead(h, stage, RING - 1)),
                send(block(h, stage, 0, hi), block(h, stage, 0, hi), ahead(h, stage, 1)),
                send(block(h, stage, 0, lo), block(h, stage, 0, lo), ahead(h, stage, RING - 1)),
            ])
        second = []
        for h in range(2):
            first[h][0].wait_recv()
            second.append(send(block(h, stage, -1, lo), block(h, stage, -1, lo), ahead(h, stage, 1)))
            first[h][1].wait_recv()
            second.append(send(block(h, stage, 1, hi), block(h, stage, 1, hi), ahead(h, stage, RING - 1)))
        for h in range(2):
            first[h][2].wait_recv()
            first[h][3].wait_recv()
        for cp in second:
            cp.wait_recv()

    for cp in loads:
        cp.wait()
    for cp in weights:
        cp.wait_recv()

    pairs = RING * RING // 2
    lanes = 2 * feat

    def pair_place(h, j):
        px, py = j // (RING // 2), j % (RING // 2) * 2
        return ((px, py), (px, py + 1)) if h == 0 else ((py, px), (py + 1, px))

    slots = half_src * cap
    for h in range(2):
        for j in range(pairs):
            (a0, b0), (a1, b1) = pair_place(h, j)
            row = slice(h * rows, (h + 1) * rows)
            base = j * lanes
            zfull[row, base:base + 128] = zbuf[h, a0, b0, :, 0:128]
            zfull[row, base + 128:base + 256] = zbuf[h, a0, b0, :, 128:256] + zbuf[h, a1, b1, :, 0:128]
            zfull[row, base + 256:base + 384] = zbuf[h, a1, b1, :, 128:256]

    chip_hid = CORES * hid
    for h in range(2):
        act = zfull[h * rows:(h + 1) * rows, :]
        gate = nn(act, wg[...]).reshape(half_src, tok, chip_hid)[:, 0:cap].reshape(slots, chip_hid)
        up = nn(act, wu[...]).reshape(half_src, tok, chip_hid)[:, 0:cap].reshape(slots, chip_hid)
        back = nt(act, wd[...]).reshape(half_src, tok, chip_hid)[:, cap:tok].reshape(slots, chip_hid)
        sig = 1.0 / (1.0 + jnp.exp(-gate))
        dgu[h * slots:(h + 1) * slots, 0:chip_hid] = (back * up * sig * (1.0 + gate * (1.0 - sig))).astype(BF16)
        dgu[h * slots:(h + 1) * slots, chip_hid:] = (back * gate * sig).astype(BF16)
    for j in range(pairs):
        part = nt(dgu[:, 0:chip_hid], wg[j * lanes:(j + 1) * lanes, :])
        part = part + nt(dgu[:, chip_hid:], wu[j * lanes:(j + 1) * lanes, :])
        part = part.astype(BF16)
        for h in range(2):
            (a0, b0), (a1, b1) = pair_place(h, j)
            sbuf[h, a0, b0] = part[h * slots:(h + 1) * slots, 0:256]
            sbuf[h, a1, b1] = part[h * slots:(h + 1) * slots, 128:384]

    slo, shi = slice(0, slots // 2), slice(slots // 2, slots)

    def add(a, b):
        return a.astype(F32) + b.astype(F32)

    first = []
    for h in range(2):
        a = place(h)[0]
        nxt, opp, prv = (a + 1) % RING, (a + 2) % RING, (a + 3) % RING
        first.append([
            send(sbuf.at[h, opp, :, slo], relay.at[h, 0], ahead(h, 0, 1)),
            send(sbuf.at[h, opp, :, shi], relay.at[h, 1], ahead(h, 0, RING - 1)),
            send(sbuf.at[h, nxt, :, shi], main.at[h, 0, :, shi], ahead(h, 0, 1)),
            send(sbuf.at[h, prv, :, slo], main.at[h, 1, :, slo], ahead(h, 0, RING - 1)),
        ])
    second = []
    for h in range(2):
        a = place(h)[0]
        nxt, prv = (a + 1) % RING, (a + 3) % RING
        first[h][0].wait_recv()
        sbuf[h, nxt, :, slo] = add(sbuf[h, nxt, :, slo], relay[h, 0]).astype(BF16)
        first[h].append(send(sbuf.at[h, nxt, :, slo], main.at[h, 0, :, slo], ahead(h, 0, 1)))
        first[h][1].wait_recv()
        sbuf[h, prv, :, shi] = add(sbuf[h, prv, :, shi], relay[h, 1]).astype(BF16)
        first[h].append(send(sbuf.at[h, prv, :, shi], main.at[h, 1, :, shi], ahead(h, 0, RING - 1)))
    second = []
    for h in range(2):
        for cp in first[h][2:]:
            cp.wait_recv()
        a, b = place(h)
        total = add(sbuf[h, a], main[h, 0]) + main[h, 1].astype(F32)
        tsum[h] = total
        thalf[h] = total.astype(BF16)
        nxt, opp, prv = (b + 1) % RING, (b + 2) % RING, (b + 3) % RING
        second.append([
            send(thalf.at[h, opp, slo], relay2.at[h, 0], ahead(h, 1, 1)),
            send(thalf.at[h, opp, shi], relay2.at[h, 1], ahead(h, 1, RING - 1)),
            send(thalf.at[h, nxt, shi], main2.at[h, 0, shi], ahead(h, 1, 1)),
            send(thalf.at[h, prv, slo], main2.at[h, 1, slo], ahead(h, 1, RING - 1)),
        ])
    for h in range(2):
        b = place(h)[1]
        nxt, prv = (b + 1) % RING, (b + 3) % RING
        second[h][0].wait_recv()
        thalf[h, nxt, slo] = (tsum[h, nxt, slo] + relay2[h, 0].astype(F32)).astype(BF16)
        second[h].append(send(thalf.at[h, nxt, slo], main2.at[h, 0, slo], ahead(h, 1, 1)))
        second[h][1].wait_recv()
        thalf[h, prv, shi] = (tsum[h, prv, shi] + relay2[h, 1].astype(F32)).astype(BF16)
        second[h].append(send(thalf.at[h, prv, shi], main2.at[h, 1, shi], ahead(h, 1, RING - 1)))
    per_zl = EXPERTS * cap
    for h in range(2):
        for cp in second[h][2:]:
            cp.wait_recv()
        b = place(h)[1]
        total = tsum[h, b] + main2[h, 0].astype(F32) + main2[h, 1].astype(F32)
        total = total.reshape(zl_n // 2, per_zl, WIN)
        fsum[h * (zl_n // 2):(h + 1) * (zl_n // 2)] = total
        fhalf[h * (zl_n // 2):(h + 1) * (zl_n // 2)] = total.astype(BF16)

    moves = []
    for d in range(1, zl_n):
        to = (zl + d) % zl_n
        moves.append(send(fhalf.at[to], zrecv.at[d - 1], at_dp(e * zl_n + to, core)))
    for cp in moves:
        cp.wait_recv()
    total = fsum[zl]
    for d in range(1, zl_n):
        total = total + zrecv[d - 1].astype(F32)
    vsum[...] = total.reshape(EXPERTS, cap, WIN)
    own = pltpu.make_async_copy(vsum.at[e], rfin.at[e], load_sem.at[3])
    own.start()
    moves = []
    for d in range(1, EXPERTS):
        to = (e + d) % EXPERTS
        moves.append(send(vsum.at[to], rfin.at[e], at_dp(to * zl_n + zl, core)))
    own.wait()
    for cp in moves:
        cp.wait_recv()
    routed = nn(placed, rfin[...].reshape(EXPERTS * cap, WIN), lax.Precision.HIGHEST)
    turned = pltpu.roll(routed, feat, 1)
    out_ref[...] = jnp.where(odd == 1, turned, routed)[:, 0:feat]
    for cp in started:
        cp.wait_send()


def solution(mesh):
    zl_n = mesh.shape["dp"] // (EXPERTS * CORES)

    def local(tokens, upstream, route_ids, route_weights, w_gate, w_up, w_down):
        tok, feat = tokens.shape
        width, hid = w_gate.shape
        cap = tok // 2
        src_n = zl_n * EXPERTS
        rows, slots = src_n * tok // 2, src_n * cap // 2
        copies = 3 + 2 * (EXPERTS - 1) + 2 * (zl_n - 1) + 48
        vmem = pl.BlockSpec(memory_space=pltpu.VMEM)
        hbm = pl.BlockSpec(memory_space=pl.ANY)
        return pl.pallas_call(
            functools.partial(kernel, zl_n),
            out_shape=jax.ShapeDtypeStruct((tok, feat), F32),
            in_specs=[vmem] * 4 + [hbm] * 3,
            out_specs=vmem,
            scratch_shapes=[
                pltpu.VMEM((width, CORES * hid), BF16),
                pltpu.VMEM((width, CORES * hid), BF16),
                pltpu.VMEM((CORES * hid, width), BF16),
                pltpu.VMEM((EXPERTS, tok, WIN), BF16),
                pltpu.VMEM((2, RING, RING, rows, WIN), BF16),
                pltpu.VMEM((2 * rows, width), BF16),
                pltpu.VMEM((2 * slots, 2 * CORES * hid), BF16),
                pltpu.VMEM((2, RING, RING, slots, WIN), BF16),
                pltpu.VMEM((2, 2, RING, slots // 2, WIN), BF16),
                pltpu.VMEM((2, 2, RING, slots, WIN), BF16),
                pltpu.VMEM((2, RING, slots, WIN), F32),
                pltpu.VMEM((2, RING, slots, WIN), BF16),
                pltpu.VMEM((2, 2, slots // 2, WIN), BF16),
                pltpu.VMEM((2, 2, slots, WIN), BF16),
                pltpu.VMEM((zl_n, EXPERTS * cap, WIN), F32),
                pltpu.VMEM((zl_n, EXPERTS * cap, WIN), BF16),
                pltpu.VMEM((zl_n - 1, EXPERTS * cap, WIN), BF16),
                pltpu.VMEM((EXPERTS, cap, WIN), F32),
                pltpu.VMEM((EXPERTS, cap, WIN), F32),
                pltpu.SemaphoreType.DMA((4,)),
                pltpu.SemaphoreType.DMA((copies,)),
                pltpu.SemaphoreType.DMA((copies,)),
            ],
            compiler_params=pltpu.CompilerParams(
                collective_id=0, has_side_effects=True, vmem_limit_bytes=48 * 1024 * 1024
            ),
        )(tokens, upstream, route_ids, route_weights, w_gate, w_up, w_down)

    in_specs = (
        P("dp", "etp"),
        P("dp", "etp"),
        P("dp", None),
        P("dp", None),
        P(None, ("dp", "etp")),
        P(None, ("dp", "etp")),
        P(("dp", "etp"), None),
    )
    return jax.shard_map(local, mesh=mesh, in_specs=in_specs, out_specs=P("dp", "etp"), check_vma=False)
```

```python
import functools

import jax
import jax.numpy as jnp
from jax import lax
from jax.experimental import pallas as pl
from jax.experimental.pallas import tpu as pltpu
from jax.sharding import PartitionSpec as P

EXPERTS = 8
CORES = 2
RING = 4
ZL = 4
LANES = 128
F32 = jnp.float32
BF16 = jnp.bfloat16
MESH = pl.DeviceIdType.MESH


def nn(a, b, precision=None):
    return lax.dot_general(a, b, (((1,), (0,)), ((), ())), preferred_element_type=F32, precision=precision)


def nt(a, b, precision=None):
    return lax.dot_general(a, b, (((1,), (1,)), ((), ())), preferred_element_type=F32, precision=precision)


def tn(a, b):
    return lax.dot_general(a, b, (((0,), (0,)), ((), ())), preferred_element_type=F32)


def kernel(
    tok_hbm, up_hbm, ids_hbm, rw_hbm, wg_hbm, wu_hbm, wd_hbm,
    out_ref,
    tok_ref, up_ref, ids_ref, rw_ref, wg, wu, wd, blk, land, pbuf, zfull, dgu,
    ssum, sbuf, relay, main, tsum, thalf, relay2, main2, fsum, fhalf, zrecv, vsum, rfin,
    load_sem, send_sem, recv_sem,
):
    tok, feat = tok_ref.shape
    cap = tok // 2
    dp, etp = lax.axis_index("dp"), lax.axis_index("etp")
    core, z = dp % CORES, dp // CORES
    zl, e = z % ZL, z // ZL
    x, y = etp // RING, etp % RING
    odd, late = etp % 2, e // (EXPERTS // 2)
    counter = [0]
    started = []

    def at_dp(zz, cc):
        return {"dp": zz * CORES + cc}

    def at_xy(xx, yy):
        return {"etp": xx * RING + yy}

    def send(src, dst, device):
        k = counter[0]
        counter[0] += 1
        cp = pltpu.make_async_remote_copy(
            src_ref=src, dst_ref=dst, send_sem=send_sem.at[k], recv_sem=recv_sem.at[k], device_id=device,
            device_id_type=MESH,
        )
        cp.start()
        started.append(cp)
        return cp

    partners = [at_dp((e + d) % EXPERTS * ZL + zl, core) for d in range(1, EXPERTS)]
    partners += [at_dp(z, 1 - core)]
    partners += [at_dp(e * ZL + (zl + d) % ZL, core) for d in range(1, ZL)]
    partners += [at_xy((x + d) % RING, y) for d in (1, RING - 1)]
    partners += [at_xy(x, (y + d) % RING) for d in (1, RING - 1)]
    barrier = pltpu.get_barrier_semaphore()
    for device in partners:
        pl.semaphore_signal(barrier, inc=1, device_id=device, device_id_type=MESH)

    hid = wg_hbm.shape[1]
    loads = [
        pltpu.make_async_copy(src, dst, load_sem.at[k])
        for k, (src, dst) in enumerate([
            (ids_hbm, ids_ref), (rw_hbm, rw_ref), (tok_hbm, tok_ref), (up_hbm, up_ref),
            (wg_hbm, wg.at[:, 0:hid]), (wu_hbm, wu.at[:, 0:hid]), (wd_hbm, wd.at[0:hid, :]),
        ])
    ]
    for cp in loads:
        cp.start()
    for cp in loads[:4]:
        cp.wait()

    slot = lax.broadcasted_iota(jnp.int32, (EXPERTS * cap, tok), 0)
    slot_e, slot_s = slot >> 3, slot & 7
    ids = ids_ref[...]
    one0 = jnp.where(ids[0:1, :] == slot_e, 1.0, 0.0).astype(F32)
    one1 = jnp.where(ids[1:2, :] == slot_e, 1.0, 0.0).astype(F32)
    earlier = lax.broadcasted_iota(jnp.int32, (tok, tok), 0) < lax.broadcasted_iota(jnp.int32, (tok, tok), 1)
    before = nn(one0 + one1, jnp.where(earlier, 1.0, 0.0).astype(F32))
    fits = jnp.where(before == slot_s.astype(F32), 1.0, 0.0).astype(F32)
    p0, p1 = one0 * fits, one1 * fits
    placed = (p0 + p1).astype(BF16)
    f = lax.broadcasted_iota(jnp.int32, (feat, 2 * LANES), 0)
    rest = feat - LANES
    even_to = f + jnp.where(f >= LANES, late * rest, 0)
    odd_to = jnp.where(f >= rest, f - rest, LANES + f + (1 - late) * rest)
    to_lane = even_to + odd * (odd_to - even_to)
    spread = jnp.where(lax.broadcasted_iota(jnp.int32, (feat, 2 * LANES), 1) == to_lane, 1.0, 0.0).astype(F32)
    spread_half = spread.astype(BF16)
    xw = nn(tok_ref[...], spread_half).astype(BF16)
    uw = nn(up_ref[...], spread_half).astype(BF16)
    rw = rw_ref[...]
    scale = jnp.sum(p0 * rw[0:1, :] + p1 * rw[1:2, :], axis=1, keepdims=True)
    xs = nn(placed, xw).reshape(EXPERTS, cap, 2 * LANES)
    ds = (scale * nn(placed, uw)).reshape(EXPERTS, cap, 2 * LANES)
    blk[...] = jnp.concatenate([xs, ds], axis=1).astype(BF16)

    pl.semaphore_wait(barrier, len(partners))

    moves = []
    for d in (4, 3, 5, 2, 6, 1, 7):
        to = (e + d) % EXPERTS
        moves.append(send(blk.at[to], land.at[e], at_dp(to * ZL + zl, core)))
    land[e] = blk[e]
    sibling = at_dp(z, 1 - core)
    for cp in loads[4:]:
        cp.wait()
    weights = [
        send(wd_hbm, wd.at[hid:, :], sibling),
        send(wg_hbm, wg.at[:, hid:], sibling),
        send(wu_hbm, wu.at[:, hid:], sibling),
    ]
    for cp in moves:
        cp.wait_recv()
    half, zp = zl // 2, zl % 2
    pa, pb = x + half * (y - x), y + half * (x - y)
    group = EXPERTS * tok
    pair_src = EXPERTS // 2
    pbuf[half, pa, pb, zp, 0:group] = land[:, :, 0:LANES].reshape(group, LANES)
    pbuf[half, pa, pb, zp, group:] = (
        land[0:pair_src, :, LANES:] + land[pair_src:, :, LANES:]
    ).reshape(group // 2, LANES)
    region = pbuf.at[half, pa, pb, zp]
    moves = [send(region, region, at_dp(e * ZL + (zl + d) % ZL, core)) for d in (2, 1, 3)]
    for cp in moves:
        cp.wait_recv()

    def ahead(h, stage, step):
        if (h == 0) == (stage == 0):
            return at_xy((x + step) % RING, y)
        return at_xy(x, (y + step) % RING)

    def place(h):
        return (x, y) if h == 0 else (y, x)

    def unit(h, da, db, q=None):
        a, b = place(h)
        ref = pbuf.at[h, (a + da) % RING, (b + db) % RING]
        return ref if q is None else ref.at[q]

    def fan(h, stage, da, db, side, q=None):
        return send(unit(h, da, db, q), unit(h, da, db, q), ahead(h, stage, side))

    left, right = RING - 1, 1
    halves = range(2)
    s0 = [[fan(h, 0, 0, 0, right, 0), fan(h, 0, 0, 0, left, 1), fan(h, 0, 0, 0, right, 1), fan(h, 0, 0, 0, left, 0)] for h in halves]
    own = [[fan(h, 1, 0, 0, right), fan(h, 1, 0, 0, left)] for h in halves]
    over = [[], []]
    for h in halves:
        s0[h][0].wait_recv()
        over[h].append(fan(h, 0, left, 0, right, 0))
        s0[h][1].wait_recv()
        over[h].append(fan(h, 0, right, 0, left, 1))
    prev, following = [], []
    for h in halves:
        s0[h][2].wait_recv()
        prev.append([fan(h, 1, left, 0, right), fan(h, 1, left, 0, left)])
        s0[h][3].wait_recv()
        following.append([fan(h, 1, right, 0, right), fan(h, 1, right, 0, left)])
    tail = []
    opposite = []
    for h in halves:
        over[h][0].wait_recv()
        over[h][1].wait_recv()
        opposite.append([fan(h, 1, 2, 0, right, 0), fan(h, 1, 2, 0, left, 1), fan(h, 1, 2, 0, right, 1), fan(h, 1, 2, 0, left, 0)])
    for h in halves:
        own[h][0].wait_recv()
        tail.append(fan(h, 1, 0, left, right))
    for h in halves:
        prev[h][1].wait_recv()
        tail.append(fan(h, 1, left, right, left))
    for h in halves:
        following[h][0].wait_recv()
        tail.append(fan(h, 1, right, left, right, 0))
        following[h][1].wait_recv()
        tail.append(fan(h, 1, right, right, left, 1))
    for h in halves:
        opposite[h][0].wait_recv()
        tail.append(fan(h, 1, 2, left, right, 0))
        opposite[h][1].wait_recv()
        tail.append(fan(h, 1, 2, right, left, 1))
    for h in halves:
        for cp in (own[h][1], prev[h][0], opposite[h][2], opposite[h][3]):
            cp.wait_recv()
    for cp in tail:
        cp.wait_recv()
    for cp in weights:
        cp.wait_recv()

    pairs = RING * RING // 2
    wide = 2 * feat

    def pair_place(h, j):
        px, py = j // (RING // 2), j % (RING // 2) * 2
        return ((px, py), (px, py + 1)) if h == 0 else ((py, px), (py + 1, px))

    def low(shape):
        return lax.broadcasted_iota(jnp.int32, shape, 1) < rest

    for h in halves:
        for j in range(pairs):
            (a0, b0), (a1, b1) = pair_place(h, j)
            base = j * wide
            for q in range(2):
                row = (2 * h + q) * group
                mid = row + group // 2
                zfull[row:row + group, base:base + LANES] = pbuf[h, a0, b0, q, 0:group]
                zfull[row:row + group, base + 2 * LANES:base + wide] = pbuf[h, a1, b1, q, 0:group]
                even_mid = pbuf[h, a0, b0, q, group:].astype(F32)
                odd_mid = pbuf[h, a1, b1, q, group:].astype(F32)
                below = low(even_mid.shape)
                zfull[row:mid, base + LANES:base + 2 * LANES] = jnp.where(below, even_mid, odd_mid).astype(BF16)
                zfull[mid:row + group, base + LANES:base + 2 * LANES] = pltpu.roll(
                    jnp.where(below, odd_mid, even_mid), rest, 1
                ).astype(BF16)

    chip_hid = CORES * hid
    src = 2 * EXPERTS
    rows, slots = src * tok, src * cap
    for h in halves:
        act = zfull[h * rows:(h + 1) * rows, :]
        gate = nn(act, wg[...]).reshape(src, tok, chip_hid)[:, 0:cap].reshape(slots, chip_hid)
        up = nn(act, wu[...]).reshape(src, tok, chip_hid)[:, 0:cap].reshape(slots, chip_hid)
        back = nt(act, wd[...]).reshape(src, tok, chip_hid)[:, cap:tok].reshape(slots, chip_hid)
        sig = 1.0 / (1.0 + jnp.exp(-gate))
        dgu[h * slots:(h + 1) * slots, 0:chip_hid] = (back * up * sig * (1.0 + gate * (1.0 - sig))).astype(BF16)
        dgu[h * slots:(h + 1) * slots, chip_hid:] = (back * gate * sig).astype(BF16)
    per_zl = EXPERTS * cap

    def keep(h, a, b, q, r0, r1, value):
        ssum[h, a, b, q, r0:r1] = value
        sbuf[h, a, b, q, r0:r1] = value.astype(BF16)

    packed = per_zl * 3 // 2
    for j in range(pairs):
        part = nt(dgu[:, 0:chip_hid], wg[j * wide:(j + 1) * wide, :])
        part = part + nt(dgu[:, chip_hid:], wu[j * wide:(j + 1) * wide, :])
        for h in halves:
            (a0, b0), (a1, b1) = pair_place(h, j)
            for q in range(2):
                here = part[(2 * h + q) * per_zl:(2 * h + q + 1) * per_zl]
                keep(h, a0, b0, q, 0, per_zl, here[:, 0:LANES])
                keep(h, a1, b1, q, 0, per_zl, here[:, 2 * LANES:])
                first = here[0:per_zl // 2, LANES:2 * LANES]
                turned = pltpu.roll(here[per_zl // 2:, LANES:2 * LANES], rest, 1)
                below = low(first.shape)
                keep(h, a0, b0, q, per_zl, packed, jnp.where(below, first, turned))
                keep(h, a1, b1, q, per_zl, packed, jnp.where(below, turned, first))

    first = []
    for h in halves:
        a = place(h)[0]
        nxt, opp, prv = (a + 1) % RING, (a + 2) % RING, (a + 3) % RING
        first.append([
            send(sbuf.at[h, opp, :, 0], relay.at[h, 0], ahead(h, 0, right)),
            send(sbuf.at[h, opp, :, 1], relay.at[h, 1], ahead(h, 0, left)),
            send(sbuf.at[h, nxt, :, 1], main.at[h, 0, :, 1], ahead(h, 0, right)),
            send(sbuf.at[h, prv, :, 0], main.at[h, 1, :, 0], ahead(h, 0, left)),
        ])
    for h in halves:
        a = place(h)[0]
        nxt, prv = (a + 1) % RING, (a + 3) % RING
        first[h][0].wait_recv()
        sbuf[h, nxt, :, 0] = (ssum[h, nxt, :, 0] + relay[h, 0].astype(F32)).astype(BF16)
        first[h].append(send(sbuf.at[h, nxt, :, 0], main.at[h, 0, :, 0], ahead(h, 0, right)))
        first[h][1].wait_recv()
        sbuf[h, prv, :, 1] = (ssum[h, prv, :, 1] + relay[h, 1].astype(F32)).astype(BF16)
        first[h].append(send(sbuf.at[h, prv, :, 1], main.at[h, 1, :, 1], ahead(h, 0, left)))
    second = []
    for h in halves:
        for cp in first[h][2:]:
            cp.wait_recv()
        a, b = place(h)
        total = ssum[h, a] + main[h, 0].astype(F32) + main[h, 1].astype(F32)
        tsum[h] = total
        thalf[h] = total.astype(BF16)
        nxt, opp, prv = (b + 1) % RING, (b + 2) % RING, (b + 3) % RING
        second.append([
            send(thalf.at[h, opp, 0], relay2.at[h, 0], ahead(h, 1, right)),
            send(thalf.at[h, opp, 1], relay2.at[h, 1], ahead(h, 1, left)),
            send(thalf.at[h, nxt, 1], main2.at[h, 0, 1], ahead(h, 1, right)),
            send(thalf.at[h, prv, 0], main2.at[h, 1, 0], ahead(h, 1, left)),
        ])
    for h in halves:
        b = place(h)[1]
        nxt, prv = (b + 1) % RING, (b + 3) % RING
        second[h][0].wait_recv()
        thalf[h, nxt, 0] = (tsum[h, nxt, 0] + relay2[h, 0].astype(F32)).astype(BF16)
        second[h].append(send(thalf.at[h, nxt, 0], main2.at[h, 0, 0], ahead(h, 1, right)))
        second[h][1].wait_recv()
        thalf[h, prv, 1] = (tsum[h, prv, 1] + relay2[h, 1].astype(F32)).astype(BF16)
        second[h].append(send(thalf.at[h, prv, 1], main2.at[h, 1, 1], ahead(h, 1, left)))
    for h in halves:
        for cp in second[h][2:]:
            cp.wait_recv()
        b = place(h)[1]
        total = tsum[h, b] + main2[h, 0].astype(F32) + main2[h, 1].astype(F32)
        fsum[2 * h:2 * h + 2] = total
        fhalf[2 * h:2 * h + 2] = total.astype(BF16)

    moves = []
    for d in (2, 1, 3):
        to = (zl + d) % ZL
        moves.append(send(fhalf.at[to], zrecv.at[d - 1], at_dp(e * ZL + to, core)))
    for cp in moves:
        cp.wait_recv()
    total = fsum[zl]
    for d in range(1, ZL):
        total = total + zrecv[d - 1].astype(F32)
    mids = total[per_zl:].reshape(EXPERTS // 2, cap, LANES)
    mids = jnp.concatenate([mids, mids], axis=0)
    vsum[...] = jnp.concatenate([total[0:per_zl].reshape(EXPERTS, cap, LANES), mids], axis=1).astype(BF16)
    moves = []
    for d in (4, 3, 5, 2, 6, 1, 7):
        to = (e + d) % EXPERTS
        moves.append(send(vsum.at[to], rfin.at[e], at_dp(to * ZL + zl, core)))
    rfin[e] = vsum[e]
    for cp in moves:
        cp.wait_recv()
    got = rfin[...].astype(F32)
    got = jnp.concatenate(
        [got[:, 0:cap].reshape(EXPERTS * cap, LANES), got[:, cap:].reshape(EXPERTS * cap, LANES)], axis=1
    )
    out_ref[...] = nt(tn(placed, got.astype(BF16)), spread, lax.Precision.HIGHEST)
    for cp in started:
        cp.wait_send()


def solution(mesh):
    def local(tokens, upstream, route_ids, route_weights, w_gate, w_up, w_down):
        tok, feat = tokens.shape
        width, hid = w_gate.shape
        cap = tok // 2
        group, per_zl = EXPERTS * tok, EXPERTS * cap
        unit, packed = group * 3 // 2, per_zl * 3 // 2
        copies = 3 + 2 * (EXPERTS - 1) + 2 * (ZL - 1) + 44 + 24
        hbm = pl.BlockSpec(memory_space=pltpu.HBM)
        return pl.pallas_call(
            kernel,
            out_shape=jax.ShapeDtypeStruct((tok, feat), F32),
            in_specs=[hbm] * 7,
            out_specs=pl.BlockSpec(memory_space=pltpu.VMEM),
            scratch_shapes=[
                pltpu.VMEM((tok, feat), BF16),
                pltpu.VMEM((tok, feat), BF16),
                pltpu.VMEM((2, tok), jnp.int32),
                pltpu.VMEM((2, tok), F32),
                pltpu.VMEM((width, CORES * hid), BF16),
                pltpu.VMEM((width, CORES * hid), BF16),
                pltpu.VMEM((CORES * hid, width), BF16),
                pltpu.VMEM((EXPERTS, tok, 2 * LANES), BF16),
                pltpu.VMEM((EXPERTS, tok, 2 * LANES), BF16),
                pltpu.VMEM((2, RING, RING, 2, unit, LANES), BF16),
                pltpu.VMEM((ZL * group, width), BF16),
                pltpu.VMEM((ZL * per_zl, 2 * CORES * hid), BF16),
                pltpu.VMEM((2, RING, RING, 2, packed, LANES), F32),
                pltpu.VMEM((2, RING, RING, 2, packed, LANES), BF16),
                pltpu.VMEM((2, 2, RING, packed, LANES), BF16),
                pltpu.VMEM((2, 2, RING, 2, packed, LANES), BF16),
                pltpu.VMEM((2, RING, 2, packed, LANES), F32),
                pltpu.VMEM((2, RING, 2, packed, LANES), BF16),
                pltpu.VMEM((2, 2, packed, LANES), BF16),
                pltpu.VMEM((2, 2, 2, packed, LANES), BF16),
                pltpu.VMEM((ZL, packed, LANES), F32),
                pltpu.VMEM((ZL, packed, LANES), BF16),
                pltpu.VMEM((ZL - 1, packed, LANES), BF16),
                pltpu.VMEM((EXPERTS, tok, LANES), BF16),
                pltpu.VMEM((EXPERTS, tok, LANES), BF16),
                pltpu.SemaphoreType.DMA((7,)),
                pltpu.SemaphoreType.DMA((copies,)),
                pltpu.SemaphoreType.DMA((copies,)),
            ],
            compiler_params=pltpu.CompilerParams(
                collective_id=0, has_side_effects=True, vmem_limit_bytes=63 * 1024 * 1024
            ),
        )(tokens, upstream, route_ids.T, route_weights.T, w_gate, w_up, w_down)

    in_specs = (
        P("dp", "etp"),
        P("dp", "etp"),
        P("dp", None),
        P("dp", None),
        P(None, ("dp", "etp")),
        P(None, ("dp", "etp")),
        P(("dp", "etp"), None),
    )
    return jax.shard_map(local, mesh=mesh, in_specs=in_specs, out_specs=P("dp", "etp"), check_vma=False)
```

```python
import functools

import jax
import jax.numpy as jnp
from jax import lax
from jax.experimental import pallas as pl
from jax.experimental.pallas import tpu as pltpu
from jax.sharding import PartitionSpec as P

EXPERTS = 8
CORES = 2
RING = 4
ZL = 4
LANES = 128
BATCHES = ((0, 1, 7, 2), (6, 3, 5, 4))
MID_HALF = [next(k // 2 for batch in BATCHES for k, b in enumerate(batch) if b == d) for d in range(EXPERTS)]
ORDER = "nnnfnfnnffnwnffnffnfnfnfnff"
F32 = jnp.float32
BF16 = jnp.bfloat16
MESH = pl.DeviceIdType.MESH


def nn(a, b, precision=None):
    return lax.dot_general(a, b, (((1,), (0,)), ((), ())), preferred_element_type=F32, precision=precision)


def nt(a, b, precision=None):
    return lax.dot_general(a, b, (((1,), (1,)), ((), ())), preferred_element_type=F32, precision=precision)


def tn(a, b):
    return lax.dot_general(a, b, (((0,), (0,)), ((), ())), preferred_element_type=F32)


def kernel(
    tok_hbm, up_hbm, ids_hbm, rw_hbm, wg_hbm, wu_hbm, wd_hbm,
    out_ref,
    tok_ref, up_ref, ids_ref, rw_ref, wg, wu, wd, blk, land, pbuf, zfull, dgu,
    ssum, sbuf, relay, main, tsum, thalf, main2, fsum, fhalf, zrecv, vsum, rfin,
    load_sem, send_sem, recv_sem,
):
    tok, feat = tok_ref.shape
    cap = tok // 2
    dp, etp = lax.axis_index("dp"), lax.axis_index("etp")
    core, z = dp % CORES, dp // CORES
    zl, e = z % ZL, z // ZL
    x, y = etp // RING, etp % RING
    odd = etp % 2
    counter = [0]
    started = []

    def at_dp(zz, cc):
        return {"dp": zz * CORES + cc}

    def at_xy(xx, yy):
        return {"etp": xx * RING + yy}

    def send(src, dst, device):
        k = counter[0]
        counter[0] += 1
        cp = pltpu.make_async_remote_copy(
            src_ref=src, dst_ref=dst, send_sem=send_sem.at[k], recv_sem=recv_sem.at[k], device_id=device,
            device_id_type=MESH,
        )
        cp.start()
        started.append(cp)
        return cp

    partners = [at_dp((e + d) % EXPERTS * ZL + zl, core) for d in range(1, EXPERTS)]
    partners += [at_dp(z, 1 - core)]
    partners += [at_dp(e * ZL + (zl + d) % ZL, core) for d in range(1, ZL)]
    partners += [at_xy((x + d) % RING, y) for d in range(1, RING)]
    partners += [at_xy(x, (y + d) % RING) for d in range(1, RING)]
    barrier = pltpu.get_barrier_semaphore()
    for device in partners:
        pl.semaphore_signal(barrier, inc=1, device_id=device, device_id_type=MESH)

    hid = wg_hbm.shape[1]
    loads = [
        pltpu.make_async_copy(src, dst, load_sem.at[k])
        for k, (src, dst) in enumerate([
            (ids_hbm, ids_ref), (rw_hbm, rw_ref), (tok_hbm, tok_ref), (up_hbm, up_ref),
            (wg_hbm, wg.at[:, 0:hid]), (wu_hbm, wu.at[:, 0:hid]), (wd_hbm, wd.at[0:hid, :]),
        ])
    ]
    for cp in loads:
        cp.start()
    for cp in loads[:4]:
        cp.wait()

    slot = lax.broadcasted_iota(jnp.int32, (EXPERTS * cap, tok), 0)
    slot_e, slot_s = (e - (slot >> 3) + EXPERTS) & (EXPERTS - 1), slot & 7
    ids = ids_ref[...]
    one0 = jnp.where(ids[0:1, :] == slot_e, 1.0, 0.0).astype(F32)
    one1 = jnp.where(ids[1:2, :] == slot_e, 1.0, 0.0).astype(F32)
    earlier = lax.broadcasted_iota(jnp.int32, (tok, tok), 0) < lax.broadcasted_iota(jnp.int32, (tok, tok), 1)
    before = nn(one0 + one1, jnp.where(earlier, 1.0, 0.0).astype(F32))
    fits = jnp.where(before == slot_s.astype(F32), 1.0, 0.0).astype(F32)
    p0, p1 = one0 * fits, one1 * fits
    placed = (p0 + p1).astype(BF16)
    rest = feat - LANES
    f = lax.broadcasted_iota(jnp.int32, (feat, 3 * LANES), 0)
    lane = lax.broadcasted_iota(jnp.int32, (feat, 3 * LANES), 1)
    odd_to = jnp.where(f >= rest, f - rest, feat + f)
    to0 = f + odd * (odd_to - f)
    even_also = jnp.where(f >= LANES, feat + f, -1)
    odd_also = jnp.where(f >= rest, -1, feat + rest + f)
    to1 = even_also + odd * (odd_also - even_also)
    spread = jnp.where(lane == to0, 1.0, 0.0).astype(F32) + jnp.where(lane == to1, 1.0, 0.0).astype(F32)
    spread_half = spread.astype(BF16)
    xw = nn(tok_ref[...], spread_half).astype(BF16)
    uw = nn(up_ref[...], spread_half).astype(BF16)
    rw = rw_ref[...]
    scale = jnp.sum(p0 * rw[0:1, :] + p1 * rw[1:2, :], axis=1, keepdims=True)
    xs = nn(placed, xw).reshape(EXPERTS, cap, 3 * LANES)
    ds = (scale * nn(placed, uw)).reshape(EXPERTS, cap, 3 * LANES)
    both = jnp.concatenate([xs, ds], axis=1).astype(BF16)
    for d in range(EXPERTS):
        blk[d, :, 0:LANES] = both[d, :, 0:LANES]
        m = LANES * (1 + MID_HALF[d])
        blk[d, :, LANES:] = both[d, :, m:m + LANES]

    pl.semaphore_wait(barrier, len(partners))

    arrive = {}
    for d in (4, 5, 3, 6, 2, 7, 1):
        arrive[d] = send(blk.at[d], land.at[d], at_dp((e - d + EXPERTS) % EXPERTS * ZL + zl, core))
    land[0] = blk[0]
    sibling = at_dp(z, 1 - core)
    for cp in loads[4:]:
        cp.wait()
    weights = [
        send(wd_hbm, wd.at[hid:, :], sibling),
        send(wg_hbm, wg.at[:, hid:], sibling),
        send(wu_hbm, wu.at[:, hid:], sibling),
    ]
    half, zp = zl // 2, zl % 2
    pa, pb = x + half * (y - x), y + half * (x - y)
    per = len(BATCHES[0])
    group, chip_hid = per * tok, CORES * hid
    left, right = RING - 1, 1
    halves = range(2)
    pairs = RING * RING // 2
    wide = 2 * feat
    src = ZL * per
    rows, slots = src * tok, src * cap
    per_zl = per * cap
    packed = per_zl * 3 // 2

    def ahead(h, stage, step):
        if (h == 0) == (stage == 0):
            return at_xy((x + step) % RING, y)
        return at_xy(x, (y + step) % RING)

    def place(h):
        return (x, y) if h == 0 else (y, x)

    def pair_place(h, j):
        px, py = j // (RING // 2), j % (RING // 2) * 2
        return ((px, py), (px, py + 1)) if h == 0 else ((py, px), (py + 1, px))

    def low(shape):
        return lax.broadcasted_iota(jnp.int32, shape, 1) < rest

    def work(n):
        batch = BATCHES[n]

        def fan(h, stage, da, db, side, q=None):
            a, b = place(h)
            ref = pbuf.at[n, h, (a + da) % RING, (b + db) % RING]
            ref = ref if q is None else ref.at[q]
            return send(ref, ref, ahead(h, stage, side))

        for d in batch:
            if d:
                arrive[d].wait_recv()
        for k, d in enumerate(batch):
            pbuf[n, half, pa, pb, zp, k * tok:(k + 1) * tok] = land[d, :, 0:LANES]
        for k in range(per // 2):
            pbuf[n, half, pa, pb, zp, group + k * tok:group + (k + 1) * tok] = (
                land[batch[k], :, LANES:] + land[batch[k + per // 2], :, LANES:]
            )
        region = pbuf.at[n, half, pa, pb, zp]
        moves = [send(region, region, at_dp(e * ZL + (zl + d) % ZL, core)) for d in (2, 1, 3)]
        yield "z"
        for cp in moves:
            cp.wait_recv()
        s0 = [[fan(h, 0, 0, 0, side) for side in (right, left, 2)] for h in halves]
        own = [[fan(h, 1, 0, 0, right), fan(h, 1, 0, 0, left)] for h in halves]
        yield "own"
        prev, following = [], []
        for h in halves:
            s0[h][0].wait_recv()
            prev.append([fan(h, 1, left, 0, right), fan(h, 1, left, 0, left)])
            s0[h][1].wait_recv()
            following.append([fan(h, 1, right, 0, right), fan(h, 1, right, 0, left)])
        yield "side"
        tail, opposite = [], []
        for h in halves:
            s0[h][2].wait_recv()
            opposite.append([fan(h, 1, 2, 0, right, 0), fan(h, 1, 2, 0, left, 1), fan(h, 1, 2, 0, right, 1), fan(h, 1, 2, 0, left, 0)])
        yield "opposite"
        for h in halves:
            own[h][0].wait_recv()
            tail.append(fan(h, 1, 0, left, right))
        for h in halves:
            prev[h][1].wait_recv()
            tail.append(fan(h, 1, left, right, left))
        yield "tail"
        for h in halves:
            following[h][0].wait_recv()
            tail.append(fan(h, 1, right, left, right, 0))
            following[h][1].wait_recv()
            tail.append(fan(h, 1, right, right, left, 1))
        for h in halves:
            opposite[h][0].wait_recv()
            tail.append(fan(h, 1, 2, left, right, 0))
            opposite[h][1].wait_recv()
            tail.append(fan(h, 1, 2, right, left, 1))
        yield "tail"
        for h in halves:
            for cp in (own[h][1], prev[h][0], opposite[h][2], opposite[h][3]):
                cp.wait_recv()
        for cp in tail:
            cp.wait_recv()
        for h in halves:
            for j in range(pairs):
                (a0, b0), (a1, b1) = pair_place(h, j)
                base = j * wide
                for q in range(2):
                    row = (2 * h + q) * group
                    mid = row + group // 2
                    zfull[n, row:row + group, base:base + LANES] = pbuf[n, h, a0, b0, q, 0:group]
                    zfull[n, row:row + group, base + 2 * LANES:base + wide] = pbuf[n, h, a1, b1, q, 0:group]
                    even_mid = pbuf[n, h, a0, b0, q, group:].astype(F32)
                    odd_mid = pbuf[n, h, a1, b1, q, group:].astype(F32)
                    below = low(even_mid.shape)
                    zfull[n, row:mid, base + LANES:base + 2 * LANES] = jnp.where(below, even_mid, odd_mid).astype(BF16)
                    zfull[n, mid:row + group, base + LANES:base + 2 * LANES] = pltpu.roll(
                        jnp.where(below, odd_mid, even_mid), rest, 1
                    ).astype(BF16)
        yield "merged"
        act = zfull[n]
        gate = nn(act, wg[...]).reshape(src, tok, chip_hid)[:, 0:cap].reshape(slots, chip_hid)
        up = nn(act, wu[...]).reshape(src, tok, chip_hid)[:, 0:cap].reshape(slots, chip_hid)
        back = nt(act, wd[...]).reshape(src, tok, chip_hid)[:, cap:tok].reshape(slots, chip_hid)
        sig = 1.0 / (1.0 + jnp.exp(-gate))
        dgu[n, :, 0:chip_hid] = (back * up * sig * (1.0 + gate * (1.0 - sig))).astype(BF16)
        dgu[n, :, chip_hid:] = (back * gate * sig).astype(BF16)
        yield "forward"

        def keep(h, a, b, q, r0, r1, value):
            ssum[n, h, a, b, q, r0:r1] = value
            sbuf[n, h, a, b, q, r0:r1] = value.astype(BF16)

        for j in range(pairs):
            part = nt(dgu[n, :, 0:chip_hid], wg[j * wide:(j + 1) * wide, :])
            part = part + nt(dgu[n, :, chip_hid:], wu[j * wide:(j + 1) * wide, :])
            for h in halves:
                (a0, b0), (a1, b1) = pair_place(h, j)
                for q in range(2):
                    here = part[(2 * h + q) * per_zl:(2 * h + q + 1) * per_zl]
                    keep(h, a0, b0, q, 0, per_zl, here[:, 0:LANES])
                    keep(h, a1, b1, q, 0, per_zl, here[:, 2 * LANES:])
                    lo = here[0:per_zl // 2, LANES:2 * LANES]
                    turned = pltpu.roll(here[per_zl // 2:, LANES:2 * LANES], rest, 1)
                    below = low(lo.shape)
                    keep(h, a0, b0, q, per_zl, packed, jnp.where(below, lo, turned))
                    keep(h, a1, b1, q, per_zl, packed, jnp.where(below, turned, lo))
        first = []
        for h in halves:
            a = place(h)[0]
            nxt, opp, prv = (a + 1) % RING, (a + 2) % RING, (a + 3) % RING
            first.append([
                send(sbuf.at[n, h, opp, :, 0], relay.at[n, h, 0], ahead(h, 0, right)),
                send(sbuf.at[n, h, opp, :, 1], relay.at[n, h, 1], ahead(h, 0, left)),
                send(sbuf.at[n, h, nxt, :, 1], main.at[n, h, 0, :, 1], ahead(h, 0, right)),
                send(sbuf.at[n, h, prv, :, 0], main.at[n, h, 1, :, 0], ahead(h, 0, left)),
            ])
        yield "backward"
        for h in halves:
            a = place(h)[0]
            nxt, prv = (a + 1) % RING, (a + 3) % RING
            first[h][0].wait_recv()
            sbuf[n, h, nxt, :, 0] = (ssum[n, h, nxt, :, 0] + relay[n, h, 0].astype(F32)).astype(BF16)
            first[h].append(send(sbuf.at[n, h, nxt, :, 0], main.at[n, h, 0, :, 0], ahead(h, 0, right)))
            first[h][1].wait_recv()
            sbuf[n, h, prv, :, 1] = (ssum[n, h, prv, :, 1] + relay[n, h, 1].astype(F32)).astype(BF16)
            first[h].append(send(sbuf.at[n, h, prv, :, 1], main.at[n, h, 1, :, 1], ahead(h, 0, left)))
        yield "relayed"
        second = []
        for h in halves:
            for cp in first[h][2:]:
                cp.wait_recv()
            a, b = place(h)
            total = ssum[n, h, a] + main[n, h, 0].astype(F32) + main[n, h, 1].astype(F32)
            tsum[n, h] = total
            thalf[n, h] = total.astype(BF16)
            second.append([
                send(thalf.at[n, h, (b + d) % RING], main2.at[n, h, d - 1], ahead(h, 1, d)) for d in (2, 1, 3)
            ])
        yield "summed"
        for h in halves:
            for cp in second[h]:
                cp.wait_recv()
            total = tsum[n, h, place(h)[1]]
            for d in range(1, RING):
                total = total + main2[n, h, d - 1].astype(F32)
            fsum[n, 2 * h:2 * h + 2] = total
            fhalf[n, 2 * h:2 * h + 2] = total.astype(BF16)
        moves = []
        for d in (2, 1, 3):
            to = (zl + d) % ZL
            moves.append(send(fhalf.at[n, to], zrecv.at[n, d - 1], at_dp(e * ZL + to, core)))
        yield "summed"
        for cp in moves:
            cp.wait_recv()
        total = fsum[n, zl]
        for d in range(1, ZL):
            total = total + zrecv[n, d - 1].astype(F32)
        mids = total[per_zl:].reshape(per // 2, cap, LANES)
        mids = jnp.concatenate([mids, mids], axis=0)
        vsum[n] = jnp.concatenate([total[0:per_zl].reshape(per, cap, LANES), mids], axis=1).astype(BF16)
        for k, d in reversed(list(enumerate(batch))):
            if d:
                returned.append(send(vsum.at[n, k], rfin.at[d], at_dp((e + d) % EXPERTS * ZL + zl, core)))
            else:
                rfin[0] = vsum[n, k]
        yield "back"

    returned = []
    near, far = work(0), work(1)
    for step in ORDER:
        if step == "w":
            for cp in weights:
                cp.wait_recv()
        else:
            next(near if step == "n" else far)
    for cp in returned:
        cp.wait_recv()
    got = rfin[...].astype(F32)
    mains, mids = got[:, 0:cap].reshape(EXPERTS * cap, LANES), got[:, cap:]
    empty = jnp.zeros((cap, LANES), F32)
    mids0 = jnp.concatenate([empty if MID_HALF[d] else mids[d] for d in range(EXPERTS)], axis=0)
    mids1 = jnp.concatenate([mids[d] if MID_HALF[d] else empty for d in range(EXPERTS)], axis=0)
    got = jnp.concatenate([mains, mids0, mids1], axis=1).astype(BF16)
    out_ref[...] = nt(tn(placed, got), spread, lax.Precision.HIGHEST)
    for cp in started:
        cp.wait_send()


def solution(mesh):
    def local(tokens, upstream, route_ids, route_weights, w_gate, w_up, w_down):
        tok, feat = tokens.shape
        width, hid = w_gate.shape
        cap = tok // 2
        per = EXPERTS // 2
        group, per_zl = per * tok, per * cap
        unit, packed = group * 3 // 2, per_zl * 3 // 2
        copies = 3 + 2 * (EXPERTS - 1) + 2 * (2 * (ZL - 1) + 38 + 18)
        hbm = pl.BlockSpec(memory_space=pltpu.HBM)
        return pl.pallas_call(
            kernel,
            out_shape=jax.ShapeDtypeStruct((tok, feat), F32),
            in_specs=[hbm] * 7,
            out_specs=pl.BlockSpec(memory_space=pltpu.VMEM),
            scratch_shapes=[
                pltpu.VMEM((tok, feat), BF16),
                pltpu.VMEM((tok, feat), BF16),
                pltpu.VMEM((2, tok), jnp.int32),
                pltpu.VMEM((2, tok), F32),
                pltpu.VMEM((width, CORES * hid), BF16),
                pltpu.VMEM((width, CORES * hid), BF16),
                pltpu.VMEM((CORES * hid, width), BF16),
                pltpu.VMEM((EXPERTS, tok, 2 * LANES), BF16),
                pltpu.VMEM((EXPERTS, tok, 2 * LANES), BF16),
                pltpu.VMEM((2, 2, RING, RING, 2, unit, LANES), BF16),
                pltpu.VMEM((2, ZL * group, width), BF16),
                pltpu.VMEM((2, ZL * per_zl, 2 * CORES * hid), BF16),
                pltpu.VMEM((2, 2, RING, RING, 2, packed, LANES), F32),
                pltpu.VMEM((2, 2, RING, RING, 2, packed, LANES), BF16),
                pltpu.VMEM((2, 2, 2, RING, packed, LANES), BF16),
                pltpu.VMEM((2, 2, 2, RING, 2, packed, LANES), BF16),
                pltpu.VMEM((2, 2, RING, 2, packed, LANES), F32),
                pltpu.VMEM((2, 2, RING, 2, packed, LANES), BF16),
                pltpu.VMEM((2, 2, RING - 1, 2, packed, LANES), BF16),
                pltpu.VMEM((2, ZL, packed, LANES), F32),
                pltpu.VMEM((2, ZL, packed, LANES), BF16),
                pltpu.VMEM((2, ZL - 1, packed, LANES), BF16),
                pltpu.VMEM((2, per, tok, LANES), BF16),
                pltpu.VMEM((EXPERTS, tok, LANES), BF16),
                pltpu.SemaphoreType.DMA((7,)),
                pltpu.SemaphoreType.DMA((copies,)),
                pltpu.SemaphoreType.DMA((copies,)),
            ],
            compiler_params=pltpu.CompilerParams(
                collective_id=0, has_side_effects=True, vmem_limit_bytes=63 * 1024 * 1024
            ),
        )(tokens, upstream, route_ids.T, route_weights.T, w_gate, w_up, w_down)

    in_specs = (
        P("dp", "etp"),
        P("dp", "etp"),
        P("dp", None),
        P("dp", None),
        P(None, ("dp", "etp")),
        P(None, ("dp", "etp")),
        P(("dp", "etp"), None),
    )
    return jax.shard_map(local, mesh=mesh, in_specs=in_specs, out_specs=P("dp", "etp"), check_vma=False)
```

```python
import functools

import jax
import jax.numpy as jnp
from jax import lax
from jax.experimental import pallas as pl
from jax.experimental.pallas import tpu as pltpu
from jax.sharding import PartitionSpec as P

EXPERTS = 8
CORES = 2
RING = 4
ZL = 4
LANES = 128
BATCHES = ((0, 1, 7, 2), (6, 3, 5, 4))
MID_HALF = [next(k // 2 for batch in BATCHES for k, b in enumerate(batch) if b == d) for d in range(EXPERTS)]
STRAIGHT = (1,)
ORDER = "nnnfnfnnffnwnffnffnfnfnfnff"
F32 = jnp.float32
BF16 = jnp.bfloat16
MESH = pl.DeviceIdType.MESH


def nn(a, b, precision=None):
    return lax.dot_general(a, b, (((1,), (0,)), ((), ())), preferred_element_type=F32, precision=precision)


def nt(a, b, precision=None):
    return lax.dot_general(a, b, (((1,), (1,)), ((), ())), preferred_element_type=F32, precision=precision)


def tn(a, b):
    return lax.dot_general(a, b, (((0,), (0,)), ((), ())), preferred_element_type=F32)


def kernel(
    tok_hbm, up_hbm, ids_hbm, rw_hbm, wg_hbm, wu_hbm, wd_hbm,
    out_ref,
    tok_ref, up_ref, ids_ref, rw_ref, wg, wu, wd, blk, land, pbuf, zfull, dgu,
    ssum, sbuf, relay, main, tsum, thalf, main2, fsum, fhalf, zrecv, vsum, rfin,
    load_sem, send_sem, recv_sem,
):
    tok, feat = tok_ref.shape
    cap = tok // 2
    dp, etp = lax.axis_index("dp"), lax.axis_index("etp")
    core, z = dp % CORES, dp // CORES
    zl, e = z % ZL, z // ZL
    x, y = etp // RING, etp % RING
    odd = etp % 2
    counter = [0]
    started = []

    def at_dp(zz, cc):
        return {"dp": zz * CORES + cc}

    def at_xy(xx, yy):
        return {"etp": xx * RING + yy}

    def send(src, dst, device):
        k = counter[0]
        counter[0] += 1
        cp = pltpu.make_async_remote_copy(
            src_ref=src, dst_ref=dst, send_sem=send_sem.at[k], recv_sem=recv_sem.at[k], device_id=device,
            device_id_type=MESH,
        )
        cp.start()
        started.append(cp)
        return cp

    partners = [at_dp((e + d) % EXPERTS * ZL + zl, core) for d in range(1, EXPERTS)]
    partners += [at_dp(z, 1 - core)]
    partners += [at_dp(e * ZL + (zl + d) % ZL, core) for d in range(1, ZL)]
    partners += [at_xy((x + d) % RING, y) for d in range(1, RING)]
    partners += [at_xy(x, (y + d) % RING) for d in range(1, RING)]
    barrier = pltpu.get_barrier_semaphore()
    for device in partners:
        pl.semaphore_signal(barrier, inc=1, device_id=device, device_id_type=MESH)

    hid = wg_hbm.shape[1]
    loads = [
        pltpu.make_async_copy(src, dst, load_sem.at[k])
        for k, (src, dst) in enumerate([
            (ids_hbm, ids_ref), (rw_hbm, rw_ref), (tok_hbm, tok_ref), (up_hbm, up_ref),
            (wg_hbm, wg.at[:, 0:hid]), (wu_hbm, wu.at[:, 0:hid]), (wd_hbm, wd.at[0:hid, :]),
        ])
    ]
    for cp in loads:
        cp.start()
    for cp in loads[:4]:
        cp.wait()

    slot = lax.broadcasted_iota(jnp.int32, (EXPERTS * cap, tok), 0)
    slot_e, slot_s = (e - (slot >> 3) + EXPERTS) & (EXPERTS - 1), slot & 7
    ids = ids_ref[...]
    one0 = jnp.where(ids[0:1, :] == slot_e, 1.0, 0.0).astype(F32)
    one1 = jnp.where(ids[1:2, :] == slot_e, 1.0, 0.0).astype(F32)
    earlier = lax.broadcasted_iota(jnp.int32, (tok, tok), 0) < lax.broadcasted_iota(jnp.int32, (tok, tok), 1)
    before = nn(one0 + one1, jnp.where(earlier, 1.0, 0.0).astype(F32))
    fits = jnp.where(before == slot_s.astype(F32), 1.0, 0.0).astype(F32)
    p0, p1 = one0 * fits, one1 * fits
    placed = (p0 + p1).astype(BF16)
    rest = feat - LANES
    f = lax.broadcasted_iota(jnp.int32, (feat, 3 * LANES), 0)
    lane = lax.broadcasted_iota(jnp.int32, (feat, 3 * LANES), 1)
    odd_to = jnp.where(f >= rest, f - rest, feat + f)
    to0 = f + odd * (odd_to - f)
    even_also = jnp.where(f >= LANES, feat + f, -1)
    odd_also = jnp.where(f >= rest, -1, feat + rest + f)
    to1 = even_also + odd * (odd_also - even_also)
    spread = jnp.where(lane == to0, 1.0, 0.0).astype(F32) + jnp.where(lane == to1, 1.0, 0.0).astype(F32)
    spread_half = spread.astype(BF16)
    xw = nn(tok_ref[...], spread_half).astype(BF16)
    uw = nn(up_ref[...], spread_half).astype(BF16)
    rw = rw_ref[...]
    scale = jnp.sum(p0 * rw[0:1, :] + p1 * rw[1:2, :], axis=1, keepdims=True)
    xs = nn(placed, xw).reshape(EXPERTS, cap, 3 * LANES)
    ds = (scale * nn(placed, uw)).reshape(EXPERTS, cap, 3 * LANES)
    both = jnp.concatenate([xs, ds], axis=1).astype(BF16)
    for d in range(EXPERTS):
        blk[d, :, 0:LANES] = both[d, :, 0:LANES]
        m = LANES * (1 + MID_HALF[d])
        blk[d, :, LANES:] = both[d, :, m:m + LANES]

    pl.semaphore_wait(barrier, len(partners))

    arrive = {}
    for d in (4, 5, 3, 6, 2, 7, 1):
        arrive[d] = send(blk.at[d], land.at[d], at_dp((e - d + EXPERTS) % EXPERTS * ZL + zl, core))
    land[0] = blk[0]
    sibling = at_dp(z, 1 - core)
    for cp in loads[4:]:
        cp.wait()
    weights = [
        send(wd_hbm, wd.at[hid:, :], sibling),
        send(wg_hbm, wg.at[:, hid:], sibling),
        send(wu_hbm, wu.at[:, hid:], sibling),
    ]
    half, zp = zl // 2, zl % 2
    pa, pb = x + half * (y - x), y + half * (x - y)
    per = len(BATCHES[0])
    group, chip_hid = per * tok, CORES * hid
    left, right = RING - 1, 1
    halves = range(2)
    pairs = RING * RING // 2
    wide = 2 * feat
    src = ZL * per
    rows, slots = src * tok, src * cap
    per_zl = per * cap
    packed = per_zl * 3 // 2

    def ahead(h, stage, step):
        if (h == 0) == (stage == 0):
            return at_xy((x + step) % RING, y)
        return at_xy(x, (y + step) % RING)

    def place(h):
        return (x, y) if h == 0 else (y, x)

    def pair_place(h, j):
        px, py = j // (RING // 2), j % (RING // 2) * 2
        return ((px, py), (px, py + 1)) if h == 0 else ((py, px), (py + 1, px))

    def low(shape):
        return lax.broadcasted_iota(jnp.int32, shape, 1) < rest

    def work(n):
        batch = BATCHES[n]

        def fan(h, stage, da, db, side, q=None):
            a, b = place(h)
            ref = pbuf.at[n, h, (a + da) % RING, (b + db) % RING]
            ref = ref if q is None else ref.at[q]
            return send(ref, ref, ahead(h, stage, side))

        for d in batch:
            if d:
                arrive[d].wait_recv()
        for k, d in enumerate(batch):
            pbuf[n, half, pa, pb, zp, k * tok:(k + 1) * tok] = land[d, :, 0:LANES]
        for k in range(per // 2):
            pbuf[n, half, pa, pb, zp, group + k * tok:group + (k + 1) * tok] = (
                land[batch[k], :, LANES:] + land[batch[k + per // 2], :, LANES:]
            )
        region = pbuf.at[n, half, pa, pb, zp]
        moves = [send(region, region, at_dp(e * ZL + (zl + d) % ZL, core)) for d in (2, 1, 3)]
        yield "z"
        for cp in moves:
            cp.wait_recv()
        s0 = [[fan(h, 0, 0, 0, side) for side in (right, left, 2)] for h in halves]
        own = [[fan(h, 1, 0, 0, right), fan(h, 1, 0, 0, left)] for h in halves]
        yield "own"
        prev, following = [], []
        for h in halves:
            s0[h][0].wait_recv()
            prev.append([fan(h, 1, left, 0, right), fan(h, 1, left, 0, left)])
            s0[h][1].wait_recv()
            following.append([fan(h, 1, right, 0, right), fan(h, 1, right, 0, left)])
        yield "side"
        tail, opposite = [], []
        for h in halves:
            s0[h][2].wait_recv()
            opposite.append([fan(h, 1, 2, 0, right, 0), fan(h, 1, 2, 0, left, 1), fan(h, 1, 2, 0, right, 1), fan(h, 1, 2, 0, left, 0)])
        yield "opposite"
        for h in halves:
            own[h][0].wait_recv()
            tail.append(fan(h, 1, 0, left, right))
        for h in halves:
            prev[h][1].wait_recv()
            tail.append(fan(h, 1, left, right, left))
        yield "tail"
        for h in halves:
            following[h][0].wait_recv()
            tail.append(fan(h, 1, right, left, right, 0))
            following[h][1].wait_recv()
            tail.append(fan(h, 1, right, right, left, 1))
        for h in halves:
            opposite[h][0].wait_recv()
            tail.append(fan(h, 1, 2, left, right, 0))
            opposite[h][1].wait_recv()
            tail.append(fan(h, 1, 2, right, left, 1))
        yield "tail"
        for h in halves:
            for cp in (own[h][1], prev[h][0], opposite[h][2], opposite[h][3]):
                cp.wait_recv()
        for cp in tail:
            cp.wait_recv()
        for h in halves:
            for j in range(pairs):
                (a0, b0), (a1, b1) = pair_place(h, j)
                base = j * wide
                for q in range(2):
                    row = (2 * h + q) * group
                    mid = row + group // 2
                    zfull[n, row:row + group, base:base + LANES] = pbuf[n, h, a0, b0, q, 0:group]
                    zfull[n, row:row + group, base + 2 * LANES:base + wide] = pbuf[n, h, a1, b1, q, 0:group]
                    even_mid = pbuf[n, h, a0, b0, q, group:].astype(F32)
                    odd_mid = pbuf[n, h, a1, b1, q, group:].astype(F32)
                    below = low(even_mid.shape)
                    zfull[n, row:mid, base + LANES:base + 2 * LANES] = jnp.where(below, even_mid, odd_mid).astype(BF16)
                    zfull[n, mid:row + group, base + LANES:base + 2 * LANES] = pltpu.roll(
                        jnp.where(below, odd_mid, even_mid), rest, 1
                    ).astype(BF16)
        yield "merged"
        act = zfull[n]
        gate = nn(act, wg[...]).reshape(src, tok, chip_hid)[:, 0:cap].reshape(slots, chip_hid)
        up = nn(act, wu[...]).reshape(src, tok, chip_hid)[:, 0:cap].reshape(slots, chip_hid)
        back = nt(act, wd[...]).reshape(src, tok, chip_hid)[:, cap:tok].reshape(slots, chip_hid)
        sig = 1.0 / (1.0 + jnp.exp(-gate))
        dgu[n, :, 0:chip_hid] = (back * up * sig * (1.0 + gate * (1.0 - sig))).astype(BF16)
        dgu[n, :, chip_hid:] = (back * gate * sig).astype(BF16)
        yield "forward"

        def keep(h, a, b, q, r0, r1, value):
            ssum[n, h, a, b, q, r0:r1] = value
            sbuf[n, h, a, b, q, r0:r1] = value.astype(BF16)

        for j in range(pairs):
            part = nt(dgu[n, :, 0:chip_hid], wg[j * wide:(j + 1) * wide, :])
            part = part + nt(dgu[n, :, chip_hid:], wu[j * wide:(j + 1) * wide, :])
            for h in halves:
                (a0, b0), (a1, b1) = pair_place(h, j)
                for q in range(2):
                    here = part[(2 * h + q) * per_zl:(2 * h + q + 1) * per_zl]
                    keep(h, a0, b0, q, 0, per_zl, here[:, 0:LANES])
                    keep(h, a1, b1, q, 0, per_zl, here[:, 2 * LANES:])
                    lo = here[0:per_zl // 2, LANES:2 * LANES]
                    turned = pltpu.roll(here[per_zl // 2:, LANES:2 * LANES], rest, 1)
                    below = low(lo.shape)
                    keep(h, a0, b0, q, per_zl, packed, jnp.where(below, lo, turned))
                    keep(h, a1, b1, q, per_zl, packed, jnp.where(below, turned, lo))
        first = []
        for h in halves:
            a = place(h)[0]
            if n in STRAIGHT:
                first.append([
                    send(sbuf.at[n, h, (a + d) % RING], main.at[n, h, d - 1], ahead(h, 0, d)) for d in (2, 1, 3)
                ])
                continue
            nxt, opp, prv = (a + 1) % RING, (a + 2) % RING, (a + 3) % RING
            first.append([
                send(sbuf.at[n, h, opp, :, 0], relay.at[n, h, 0], ahead(h, 0, right)),
                send(sbuf.at[n, h, opp, :, 1], relay.at[n, h, 1], ahead(h, 0, left)),
                send(sbuf.at[n, h, nxt, :, 1], main.at[n, h, 0, :, 1], ahead(h, 0, right)),
                send(sbuf.at[n, h, prv, :, 0], main.at[n, h, 2, :, 0], ahead(h, 0, left)),
            ])
        yield "backward"
        for h in halves:
            if n in STRAIGHT:
                continue
            a = place(h)[0]
            nxt, prv = (a + 1) % RING, (a + 3) % RING
            first[h][0].wait_recv()
            sbuf[n, h, nxt, :, 0] = (ssum[n, h, nxt, :, 0] + relay[n, h, 0].astype(F32)).astype(BF16)
            first[h].append(send(sbuf.at[n, h, nxt, :, 0], main.at[n, h, 0, :, 0], ahead(h, 0, right)))
            first[h][1].wait_recv()
            sbuf[n, h, prv, :, 1] = (ssum[n, h, prv, :, 1] + relay[n, h, 1].astype(F32)).astype(BF16)
            first[h].append(send(sbuf.at[n, h, prv, :, 1], main.at[n, h, 2, :, 1], ahead(h, 0, left)))
        yield "relayed"
        second = []
        for h in halves:
            for cp in first[h][0 if n in STRAIGHT else 2:]:
                cp.wait_recv()
            a, b = place(h)
            total = ssum[n, h, a] + main[n, h, 0].astype(F32) + main[n, h, 2].astype(F32)
            if n in STRAIGHT:
                total = total + main[n, h, 1].astype(F32)
            tsum[n, h] = total
            thalf[n, h] = total.astype(BF16)
            second.append([
                send(thalf.at[n, h, (b + d) % RING], main2.at[n, h, d - 1], ahead(h, 1, d)) for d in (2, 1, 3)
            ])
        yield "summed"
        for h in halves:
            for cp in second[h]:
                cp.wait_recv()
            total = tsum[n, h, place(h)[1]]
            for d in range(1, RING):
                total = total + main2[n, h, d - 1].astype(F32)
            fsum[n, 2 * h:2 * h + 2] = total
            fhalf[n, 2 * h:2 * h + 2] = total.astype(BF16)
        moves = []
        for d in (2, 1, 3):
            to = (zl + d) % ZL
            moves.append(send(fhalf.at[n, to], zrecv.at[n, d - 1], at_dp(e * ZL + to, core)))
        yield "summed"
        for cp in moves:
            cp.wait_recv()
        total = fsum[n, zl]
        for d in range(1, ZL):
            total = total + zrecv[n, d - 1].astype(F32)
        mids = total[per_zl:].reshape(per // 2, cap, LANES)
        mids = jnp.concatenate([mids, mids], axis=0)
        vsum[n] = jnp.concatenate([total[0:per_zl].reshape(per, cap, LANES), mids], axis=1).astype(BF16)
        for k, d in reversed(list(enumerate(batch))):
            if d:
                returned.append(send(vsum.at[n, k], rfin.at[d], at_dp((e + d) % EXPERTS * ZL + zl, core)))
            else:
                rfin[0] = vsum[n, k]
        yield "back"

    returned = []
    near, far = work(0), work(1)
    for step in ORDER:
        if step == "w":
            for cp in weights:
                cp.wait_recv()
        else:
            next(near if step == "n" else far)
    for cp in started:
        if all(cp is not back for back in returned):
            cp.wait_send()
    for cp in returned:
        cp.wait_recv()
    got = rfin[...].astype(F32)
    mains, mids = got[:, 0:cap].reshape(EXPERTS * cap, LANES), got[:, cap:]
    empty = jnp.zeros((cap, LANES), F32)
    mids0 = jnp.concatenate([empty if MID_HALF[d] else mids[d] for d in range(EXPERTS)], axis=0)
    mids1 = jnp.concatenate([mids[d] if MID_HALF[d] else empty for d in range(EXPERTS)], axis=0)
    got = jnp.concatenate([mains, mids0, mids1], axis=1).astype(BF16)
    out_ref[...] = nt(tn(placed, got), spread, lax.Precision.HIGHEST)
    for cp in returned:
        cp.wait_send()


def solution(mesh):
    def local(tokens, upstream, route_ids, route_weights, w_gate, w_up, w_down):
        tok, feat = tokens.shape
        width, hid = w_gate.shape
        cap = tok // 2
        per = EXPERTS // 2
        group, per_zl = per * tok, per * cap
        unit, packed = group * 3 // 2, per_zl * 3 // 2
        copies = 3 + 2 * (EXPERTS - 1) + 2 * (2 * (ZL - 1) + 38 + 18)
        hbm = pl.BlockSpec(memory_space=pltpu.HBM)
        return pl.pallas_call(
            kernel,
            out_shape=jax.ShapeDtypeStruct((tok, feat), F32),
            in_specs=[hbm] * 7,
            out_specs=pl.BlockSpec(memory_space=pltpu.VMEM),
            scratch_shapes=[
                pltpu.VMEM((tok, feat), BF16),
                pltpu.VMEM((tok, feat), BF16),
                pltpu.VMEM((2, tok), jnp.int32),
                pltpu.VMEM((2, tok), F32),
                pltpu.VMEM((width, CORES * hid), BF16),
                pltpu.VMEM((width, CORES * hid), BF16),
                pltpu.VMEM((CORES * hid, width), BF16),
                pltpu.VMEM((EXPERTS, tok, 2 * LANES), BF16),
                pltpu.VMEM((EXPERTS, tok, 2 * LANES), BF16),
                pltpu.VMEM((2, 2, RING, RING, 2, unit, LANES), BF16),
                pltpu.VMEM((2, ZL * group, width), BF16),
                pltpu.VMEM((2, ZL * per_zl, 2 * CORES * hid), BF16),
                pltpu.VMEM((2, 2, RING, RING, 2, packed, LANES), F32),
                pltpu.VMEM((2, 2, RING, RING, 2, packed, LANES), BF16),
                pltpu.VMEM((2, 2, 2, RING, packed, LANES), BF16),
                pltpu.VMEM((2, 2, RING - 1, RING, 2, packed, LANES), BF16),
                pltpu.VMEM((2, 2, RING, 2, packed, LANES), F32),
                pltpu.VMEM((2, 2, RING, 2, packed, LANES), BF16),
                pltpu.VMEM((2, 2, RING - 1, 2, packed, LANES), BF16),
                pltpu.VMEM((2, ZL, packed, LANES), F32),
                pltpu.VMEM((2, ZL, packed, LANES), BF16),
                pltpu.VMEM((2, ZL - 1, packed, LANES), BF16),
                pltpu.VMEM((2, per, tok, LANES), BF16),
                pltpu.VMEM((EXPERTS, tok, LANES), BF16),
                pltpu.SemaphoreType.DMA((7,)),
                pltpu.SemaphoreType.DMA((copies,)),
                pltpu.SemaphoreType.DMA((copies,)),
            ],
            compiler_params=pltpu.CompilerParams(
                collective_id=0, has_side_effects=True, vmem_limit_bytes=63 * 1024 * 1024
            ),
        )(tokens, upstream, route_ids.T, route_weights.T, w_gate, w_up, w_down)

    in_specs = (
        P("dp", "etp"),
        P("dp", "etp"),
        P("dp", None),
        P("dp", None),
        P(None, ("dp", "etp")),
        P(None, ("dp", "etp")),
        P(("dp", "etp"), None),
    )
    return jax.shard_map(local, mesh=mesh, in_specs=in_specs, out_specs=P("dp", "etp"), check_vma=False)
```

```python
import functools

import jax
import jax.numpy as jnp
from jax import lax
from jax.experimental import pallas as pl
from jax.experimental.pallas import tpu as pltpu
from jax.sharding import PartitionSpec as P

EXPERTS = 8
CORES = 2
RING = 4
ZL = 4
LANES = 128
BATCHES = ((0, 1, 7, 2), (6, 3, 5, 4))
MID_HALF = [next(k // 2 for batch in BATCHES for k, b in enumerate(batch) if b == d) for d in range(EXPERTS)]
STRAIGHT = (1,)
ORDER = "nnnfnfnnffnwnffnffnfnfnfnff"
F32 = jnp.float32
BF16 = jnp.bfloat16
MESH = pl.DeviceIdType.MESH


def nn(a, b, precision=None):
    return lax.dot_general(a, b, (((1,), (0,)), ((), ())), preferred_element_type=F32, precision=precision)


def nt(a, b, precision=None):
    return lax.dot_general(a, b, (((1,), (1,)), ((), ())), preferred_element_type=F32, precision=precision)


def tn(a, b):
    return lax.dot_general(a, b, (((0,), (0,)), ((), ())), preferred_element_type=F32)


def kernel(
    tok_hbm, up_hbm, ids_hbm, rw_hbm, wg_hbm, wu_hbm, wd_hbm,
    out_ref,
    tok_ref, up_ref, ids_ref, rw_ref, wg, wu, wd, blk, land, pbuf, zfull, dgu,
    ssum, sbuf, relay, main, tsum, thalf, main2, fsum, fhalf, zrecv, vsum, rfin,
    load_sem, send_sem, recv_sem,
):
    tok, feat = tok_ref.shape
    cap = tok // 2
    dp, etp = lax.axis_index("dp"), lax.axis_index("etp")
    core, z = dp % CORES, dp // CORES
    zl, e = z % ZL, z // ZL
    x, y = etp // RING, etp % RING
    odd = etp % 2
    counter = [0]
    started = []

    def at_dp(zz, cc):
        return {"dp": zz * CORES + cc}

    def at_xy(xx, yy):
        return {"etp": xx * RING + yy}

    def send(src, dst, device):
        k = counter[0]
        counter[0] += 1
        cp = pltpu.make_async_remote_copy(
            src_ref=src, dst_ref=dst, send_sem=send_sem.at[k], recv_sem=recv_sem.at[k], device_id=device,
            device_id_type=MESH,
        )
        cp.start()
        started.append(cp)
        return cp

    partners = [at_dp((e + d) % EXPERTS * ZL + zl, core) for d in (4, 5, 3, 6, 2, 7, 1)]
    partners += [at_dp(z, 1 - core)]
    partners += [at_dp(e * ZL + (zl + d) % ZL, core) for d in range(1, ZL)]
    partners += [at_xy((x + d) % RING, y) for d in range(1, RING)]
    partners += [at_xy(x, (y + d) % RING) for d in range(1, RING)]
    barrier = pltpu.get_barrier_semaphore()
    for device in partners:
        pl.semaphore_signal(barrier, inc=1, device_id=device, device_id_type=MESH)

    hid = wg_hbm.shape[1]
    loads = [
        pltpu.make_async_copy(src, dst, load_sem.at[k])
        for k, (src, dst) in enumerate([
            (ids_hbm, ids_ref), (rw_hbm, rw_ref), (tok_hbm, tok_ref), (up_hbm, up_ref),
            (wg_hbm, wg.at[:, 0:hid]), (wu_hbm, wu.at[:, 0:hid]), (wd_hbm, wd.at[0:hid, :]),
        ])
    ]
    for cp in loads:
        cp.start()

    slot = lax.broadcasted_iota(jnp.int32, (EXPERTS * cap, tok), 0)
    slot_e, slot_s = (e - (slot >> 3) + EXPERTS) & (EXPERTS - 1), slot & 7
    earlier = lax.broadcasted_iota(jnp.int32, (tok, tok), 0) < lax.broadcasted_iota(jnp.int32, (tok, tok), 1)
    rest = feat - LANES
    f = lax.broadcasted_iota(jnp.int32, (feat, 3 * LANES), 0)
    lane = lax.broadcasted_iota(jnp.int32, (feat, 3 * LANES), 1)
    odd_to = jnp.where(f >= rest, f - rest, feat + f)
    to0 = f + odd * (odd_to - f)
    even_also = jnp.where(f >= LANES, feat + f, -1)
    odd_also = jnp.where(f >= rest, -1, feat + rest + f)
    to1 = even_also + odd * (odd_also - even_also)
    spread = jnp.where(lane == to0, 1.0, 0.0).astype(F32) + jnp.where(lane == to1, 1.0, 0.0).astype(F32)
    spread_half = spread.astype(BF16)
    for cp in loads[:4]:
        cp.wait()
    ids = ids_ref[...]
    one0 = jnp.where(ids[0:1, :] == slot_e, 1.0, 0.0).astype(F32)
    one1 = jnp.where(ids[1:2, :] == slot_e, 1.0, 0.0).astype(F32)
    before = nn(one0 + one1, jnp.where(earlier, 1.0, 0.0).astype(F32))
    fits = jnp.where(before == slot_s.astype(F32), 1.0, 0.0).astype(F32)
    p0, p1 = one0 * fits, one1 * fits
    placed = (p0 + p1).astype(BF16)
    xw = nn(tok_ref[...], spread_half).astype(BF16)
    uw = nn(up_ref[...], spread_half).astype(BF16)
    rw = rw_ref[...]
    scale = jnp.sum(p0 * rw[0:1, :] + p1 * rw[1:2, :], axis=1, keepdims=True)
    xs = nn(placed, xw).reshape(EXPERTS, cap, 3 * LANES)
    ds = (scale * nn(placed, uw)).reshape(EXPERTS, cap, 3 * LANES)
    both = jnp.concatenate([xs, ds], axis=1).astype(BF16)
    for d in range(EXPERTS):
        blk[d, :, 0:LANES] = both[d, :, 0:LANES]
        m = LANES * (1 + MID_HALF[d])
        blk[d, :, LANES:] = both[d, :, m:m + LANES]

    pl.semaphore_wait(barrier, len(partners))

    arrive = {}
    for d in (4, 5, 3, 6, 2, 7, 1):
        arrive[d] = send(blk.at[d], land.at[d], at_dp((e - d + EXPERTS) % EXPERTS * ZL + zl, core))
    land[0] = blk[0]
    sibling = at_dp(z, 1 - core)
    for cp in loads[4:]:
        cp.wait()
    weights = [
        send(wd_hbm, wd.at[hid:, :], sibling),
        send(wg_hbm, wg.at[:, hid:], sibling),
        send(wu_hbm, wu.at[:, hid:], sibling),
    ]
    half, zp = zl // 2, zl % 2
    pa, pb = x + half * (y - x), y + half * (x - y)
    per = len(BATCHES[0])
    group, chip_hid = per * tok, CORES * hid
    left, right = RING - 1, 1
    halves = range(2)
    pairs = RING * RING // 2
    wide = 2 * feat
    src = ZL * per
    rows, slots = src * tok, src * cap
    per_zl = per * cap
    packed = per_zl * 3 // 2

    def ahead(h, stage, step):
        if (h == 0) == (stage == 0):
            return at_xy((x + step) % RING, y)
        return at_xy(x, (y + step) % RING)

    def place(h):
        return (x, y) if h == 0 else (y, x)

    def pair_place(h, j):
        px, py = j // (RING // 2), j % (RING // 2) * 2
        return ((px, py), (px, py + 1)) if h == 0 else ((py, px), (py + 1, px))

    def low(shape):
        return lax.broadcasted_iota(jnp.int32, shape, 1) < rest

    def work(n):
        batch = BATCHES[n]

        def fan(h, stage, da, db, side, q=None):
            a, b = place(h)
            ref = pbuf.at[n, h, (a + da) % RING, (b + db) % RING]
            ref = ref if q is None else ref.at[q]
            return send(ref, ref, ahead(h, stage, side))

        for d in batch:
            if d:
                arrive[d].wait_recv()
        for k, d in enumerate(batch):
            pbuf[n, half, pa, pb, zp, k * tok:(k + 1) * tok] = land[d, :, 0:LANES]
        for k in range(per // 2):
            pbuf[n, half, pa, pb, zp, group + k * tok:group + (k + 1) * tok] = (
                land[batch[k], :, LANES:] + land[batch[k + per // 2], :, LANES:]
            )
        region = pbuf.at[n, half, pa, pb, zp]
        moves = [send(region, region, at_dp(e * ZL + (zl + d) % ZL, core)) for d in (2, 1, 3)]
        yield "z"
        for cp in moves:
            cp.wait_recv()
        s0 = [[fan(h, 0, 0, 0, side) for side in (right, left, 2)] for h in halves]
        own = [[fan(h, 1, 0, 0, right), fan(h, 1, 0, 0, left)] for h in halves]
        yield "own"
        prev, following = [], []
        for h in halves:
            s0[h][0].wait_recv()
            prev.append([fan(h, 1, left, 0, right), fan(h, 1, left, 0, left)])
            s0[h][1].wait_recv()
            following.append([fan(h, 1, right, 0, right), fan(h, 1, right, 0, left)])
        yield "side"
        tail, opposite = [], []
        for h in halves:
            s0[h][2].wait_recv()
            opposite.append([fan(h, 1, 2, 0, right, 0), fan(h, 1, 2, 0, left, 1), fan(h, 1, 2, 0, right, 1), fan(h, 1, 2, 0, left, 0)])
        yield "opposite"
        for h in halves:
            own[h][0].wait_recv()
            tail.append(fan(h, 1, 0, left, right))
        for h in halves:
            prev[h][1].wait_recv()
            tail.append(fan(h, 1, left, right, left))
        yield "tail"
        for h in halves:
            following[h][0].wait_recv()
            tail.append(fan(h, 1, right, left, right, 0))
            following[h][1].wait_recv()
            tail.append(fan(h, 1, right, right, left, 1))
        for h in halves:
            opposite[h][0].wait_recv()
            tail.append(fan(h, 1, 2, left, right, 0))
            opposite[h][1].wait_recv()
            tail.append(fan(h, 1, 2, right, left, 1))
        yield "tail"
        for h in halves:
            for cp in (own[h][1], prev[h][0], opposite[h][2], opposite[h][3]):
                cp.wait_recv()
        for cp in tail:
            cp.wait_recv()
        for h in halves:
            for j in range(pairs):
                (a0, b0), (a1, b1) = pair_place(h, j)
                base = j * wide
                for q in range(2):
                    row = (2 * h + q) * group
                    mid = row + group // 2
                    zfull[n, row:row + group, base:base + LANES] = pbuf[n, h, a0, b0, q, 0:group]
                    zfull[n, row:row + group, base + 2 * LANES:base + wide] = pbuf[n, h, a1, b1, q, 0:group]
                    even_mid = pbuf[n, h, a0, b0, q, group:].astype(F32)
                    odd_mid = pbuf[n, h, a1, b1, q, group:].astype(F32)
                    below = low(even_mid.shape)
                    zfull[n, row:mid, base + LANES:base + 2 * LANES] = jnp.where(below, even_mid, odd_mid).astype(BF16)
                    zfull[n, mid:row + group, base + LANES:base + 2 * LANES] = pltpu.roll(
                        jnp.where(below, odd_mid, even_mid), rest, 1
                    ).astype(BF16)
        yield "merged"
        act = zfull[n]
        gate = nn(act, wg[...]).reshape(src, tok, chip_hid)[:, 0:cap].reshape(slots, chip_hid)
        up = nn(act, wu[...]).reshape(src, tok, chip_hid)[:, 0:cap].reshape(slots, chip_hid)
        back = nt(act, wd[...]).reshape(src, tok, chip_hid)[:, cap:tok].reshape(slots, chip_hid)
        sig = 1.0 / (1.0 + jnp.exp(-gate))
        dgu[n, :, 0:chip_hid] = (back * up * sig * (1.0 + gate * (1.0 - sig))).astype(BF16)
        dgu[n, :, chip_hid:] = (back * gate * sig).astype(BF16)
        yield "forward"

        def keep(h, a, b, q, r0, r1, value):
            ssum[n, h, a, b, q, r0:r1] = value
            sbuf[n, h, a, b, q, r0:r1] = value.astype(BF16)

        for j in range(pairs):
            part = nt(dgu[n, :, 0:chip_hid], wg[j * wide:(j + 1) * wide, :])
            part = part + nt(dgu[n, :, chip_hid:], wu[j * wide:(j + 1) * wide, :])
            for h in halves:
                (a0, b0), (a1, b1) = pair_place(h, j)
                for q in range(2):
                    here = part[(2 * h + q) * per_zl:(2 * h + q + 1) * per_zl]
                    keep(h, a0, b0, q, 0, per_zl, here[:, 0:LANES])
                    keep(h, a1, b1, q, 0, per_zl, here[:, 2 * LANES:])
                    lo = here[0:per_zl // 2, LANES:2 * LANES]
                    turned = pltpu.roll(here[per_zl // 2:, LANES:2 * LANES], rest, 1)
                    below = low(lo.shape)
                    keep(h, a0, b0, q, per_zl, packed, jnp.where(below, lo, turned))
                    keep(h, a1, b1, q, per_zl, packed, jnp.where(below, turned, lo))
        first = []
        for h in halves:
            a = place(h)[0]
            if n in STRAIGHT:
                first.append([
                    send(sbuf.at[n, h, (a + d) % RING], main.at[n, h, d - 1], ahead(h, 0, d)) for d in (2, 1, 3)
                ])
                continue
            nxt, opp, prv = (a + 1) % RING, (a + 2) % RING, (a + 3) % RING
            first.append([
                send(sbuf.at[n, h, opp, :, 0], relay.at[n, h, 0], ahead(h, 0, right)),
                send(sbuf.at[n, h, opp, :, 1], relay.at[n, h, 1], ahead(h, 0, left)),
                send(sbuf.at[n, h, nxt, :, 1], main.at[n, h, 0, :, 1], ahead(h, 0, right)),
                send(sbuf.at[n, h, prv, :, 0], main.at[n, h, 2, :, 0], ahead(h, 0, left)),
            ])
        yield "backward"
        for h in halves:
            if n in STRAIGHT:
                continue
            a = place(h)[0]
            nxt, prv = (a + 1) % RING, (a + 3) % RING
            first[h][0].wait_recv()
            sbuf[n, h, nxt, :, 0] = (ssum[n, h, nxt, :, 0] + relay[n, h, 0].astype(F32)).astype(BF16)
            first[h].append(send(sbuf.at[n, h, nxt, :, 0], main.at[n, h, 0, :, 0], ahead(h, 0, right)))
            first[h][1].wait_recv()
            sbuf[n, h, prv, :, 1] = (ssum[n, h, prv, :, 1] + relay[n, h, 1].astype(F32)).astype(BF16)
            first[h].append(send(sbuf.at[n, h, prv, :, 1], main.at[n, h, 2, :, 1], ahead(h, 0, left)))
        yield "relayed"
        second = []
        for h in halves:
            for cp in first[h][0 if n in STRAIGHT else 2:]:
                cp.wait_recv()
            a, b = place(h)
            total = ssum[n, h, a] + main[n, h, 0].astype(F32) + main[n, h, 2].astype(F32)
            if n in STRAIGHT:
                total = total + main[n, h, 1].astype(F32)
            tsum[n, h] = total
            thalf[n, h] = total.astype(BF16)
            second.append([
                send(thalf.at[n, h, (b + d) % RING], main2.at[n, h, d - 1], ahead(h, 1, d)) for d in (2, 1, 3)
            ])
        yield "summed"
        for h in halves:
            for cp in second[h]:
                cp.wait_recv()
            total = tsum[n, h, place(h)[1]]
            for d in range(1, RING):
                total = total + main2[n, h, d - 1].astype(F32)
            fsum[n, 2 * h:2 * h + 2] = total
            fhalf[n, 2 * h:2 * h + 2] = total.astype(BF16)
        moves = []
        for d in (2, 1, 3):
            to = (zl + d) % ZL
            moves.append(send(fhalf.at[n, to], zrecv.at[n, d - 1], at_dp(e * ZL + to, core)))
        yield "summed"
        for cp in moves:
            cp.wait_recv()
        total = fsum[n, zl]
        for d in range(1, ZL):
            total = total + zrecv[n, d - 1].astype(F32)
        mids = total[per_zl:].reshape(per // 2, cap, LANES)
        mids = jnp.concatenate([mids, mids], axis=0)
        vsum[n] = jnp.concatenate([total[0:per_zl].reshape(per, cap, LANES), mids], axis=1).astype(BF16)
        for k, d in reversed(list(enumerate(batch))):
            if d:
                returned.append(send(vsum.at[n, k], rfin.at[d], at_dp((e + d) % EXPERTS * ZL + zl, core)))
            else:
                rfin[0] = vsum[n, k]
        yield "back"

    returned = []
    near, far = work(0), work(1)
    for step in ORDER:
        if step == "w":
            for cp in weights:
                cp.wait_recv()
        else:
            next(near if step == "n" else far)
    for cp in started:
        if all(cp is not back for back in returned):
            cp.wait_send()
    for cp in returned:
        cp.wait_recv()
    got = rfin[...].astype(F32)
    mains, mids = got[:, 0:cap].reshape(EXPERTS * cap, LANES), got[:, cap:]
    empty = jnp.zeros((cap, LANES), F32)
    mids0 = jnp.concatenate([empty if MID_HALF[d] else mids[d] for d in range(EXPERTS)], axis=0)
    mids1 = jnp.concatenate([mids[d] if MID_HALF[d] else empty for d in range(EXPERTS)], axis=0)
    got = jnp.concatenate([mains, mids0, mids1], axis=1).astype(BF16)
    out_ref[...] = nt(tn(placed, got), spread, lax.Precision.HIGHEST)
    for cp in returned:
        cp.wait_send()


def solution(mesh):
    def local(tokens, upstream, route_ids, route_weights, w_gate, w_up, w_down):
        tok, feat = tokens.shape
        width, hid = w_gate.shape
        cap = tok // 2
        per = EXPERTS // 2
        group, per_zl = per * tok, per * cap
        unit, packed = group * 3 // 2, per_zl * 3 // 2
        copies = 3 + 2 * (EXPERTS - 1) + 2 * (2 * (ZL - 1) + 38 + 18)
        hbm = pl.BlockSpec(memory_space=pltpu.HBM)
        return pl.pallas_call(
            kernel,
            out_shape=jax.ShapeDtypeStruct((tok, feat), F32),
            in_specs=[hbm] * 7,
            out_specs=pl.BlockSpec(memory_space=pltpu.VMEM),
            scratch_shapes=[
                pltpu.VMEM((tok, feat), BF16),
                pltpu.VMEM((tok, feat), BF16),
                pltpu.VMEM((2, tok), jnp.int32),
                pltpu.VMEM((2, tok), F32),
                pltpu.VMEM((width, CORES * hid), BF16),
                pltpu.VMEM((width, CORES * hid), BF16),
                pltpu.VMEM((CORES * hid, width), BF16),
                pltpu.VMEM((EXPERTS, tok, 2 * LANES), BF16),
                pltpu.VMEM((EXPERTS, tok, 2 * LANES), BF16),
                pltpu.VMEM((2, 2, RING, RING, 2, unit, LANES), BF16),
                pltpu.VMEM((2, ZL * group, width), BF16),
                pltpu.VMEM((2, ZL * per_zl, 2 * CORES * hid), BF16),
                pltpu.VMEM((2, 2, RING, RING, 2, packed, LANES), F32),
                pltpu.VMEM((2, 2, RING, RING, 2, packed, LANES), BF16),
                pltpu.VMEM((2, 2, 2, RING, packed, LANES), BF16),
                pltpu.VMEM((2, 2, RING - 1, RING, 2, packed, LANES), BF16),
                pltpu.VMEM((2, 2, RING, 2, packed, LANES), F32),
                pltpu.VMEM((2, 2, RING, 2, packed, LANES), BF16),
                pltpu.VMEM((2, 2, RING - 1, 2, packed, LANES), BF16),
                pltpu.VMEM((2, ZL, packed, LANES), F32),
                pltpu.VMEM((2, ZL, packed, LANES), BF16),
                pltpu.VMEM((2, ZL - 1, packed, LANES), BF16),
                pltpu.VMEM((2, per, tok, LANES), BF16),
                pltpu.VMEM((EXPERTS, tok, LANES), BF16),
                pltpu.SemaphoreType.DMA((7,)),
                pltpu.SemaphoreType.DMA((copies,)),
                pltpu.SemaphoreType.DMA((copies,)),
            ],
            compiler_params=pltpu.CompilerParams(
                collective_id=0, has_side_effects=True, vmem_limit_bytes=63 * 1024 * 1024
            ),
        )(tokens, upstream, route_ids.T, route_weights.T, w_gate, w_up, w_down)

    in_specs = (
        P("dp", "etp"),
        P("dp", "etp"),
        P("dp", None),
        P("dp", None),
        P(None, ("dp", "etp")),
        P(None, ("dp", "etp")),
        P(("dp", "etp"), None),
    )
    return jax.shard_map(local, mesh=mesh, in_specs=in_specs, out_specs=P("dp", "etp"), check_vma=False)
```
